256 devices in a mesh: prow: 16 (over z, core), pcol: 16 (over y, x).
Axes of the slice: x: 4, y: 4, z: 8, core: 2. Of those that a mesh axis runs over, the one named last changes fastest.
Arguments:
- matrix: float32 [16384, 24576], P('prow', 'pcol'), may hold values from -4 to 4, as said below
Outputs:
- factored: float32 [16384, 24576], P('prow', 'pcol')
- t_factor: float32 [128, 128], replicated
The draws below stay inside these ranges and needn't reach their ends.
Inputs may be any that keep to these rules, and one draw needn't show every extreme that they name: `matrix`: the panel has full column rank, and the diagonal entries of the top 128 x 128 block of orthogonal are 0.4 or more.
All inputs are finite; a program needn't handle non-finite values.
Results may differ from the reference program's by a relative error of at most 0.0003.
Values sent between devices are 32-bit elements; how exact they have to be, the bound alone decides.
A program may use at most 64 MiB of HBM per device.

```python
import math
import jax
import jax.numpy as jnp
from jax import lax

B = 128
ROWS = 16384
COLS = 24576


def draw_matrix(key, part):
    keys = jax.random.split(key, 5)
    panel_noise = jax.random.normal(keys[0], (ROWS, B), jnp.float32)
    rest_noise = jax.random.normal(keys[4], (ROWS, COLS - B), jnp.float32)
    row_scale = jnp.exp(jax.random.uniform(keys[1], (ROWS, 1), jnp.float32, 0.0, math.log(10.0)))
    row_ids = jnp.arange(ROWS)[:, None]
    col_ids = jnp.arange(B)[None, :]
    diagonal_part = jnp.where(row_ids == col_ids, 2.5, 0.0)
    top_value = diagonal_part + 0.8 / B ** 0.5 * panel_noise
    lower_value = 0.35 / ROWS ** 0.5 * row_scale * panel_noise
    panel_value = jnp.where(row_ids < B, top_value, lower_value)
    rest_value = 1.5 * jnp.sqrt(row_scale) * rest_noise
    whole = jnp.concatenate([panel_value, rest_value], axis=1)
    return jnp.clip(whole, -4.0, 4.0).astype(jnp.float32)


def setup_inputs(seed: int = 0) -> dict:
    key_list = jax.random.split(jax.random.key(seed), 2)
    matrix = draw_matrix(jax.random.fold_in(key_list[1], 71), 0)
    return dict(matrix=matrix)


def product(left, right):
    return jnp.dot(left, right, precision=lax.Precision.HIGHEST)

def small_factors(square):
    order = square.shape[0]
    position = jnp.arange(order)

    def advance(level, packed):
        pivot_value = packed[level, level]
        column = jnp.where(position > level, packed[:, level] / pivot_value, 0.0)
        pivot_row = jnp.where(position > level, packed[level, :], 0.0)
        packed = packed - column[:, None] * pivot_row[None, :]
        return packed.at[:, level].set(jnp.where(position > level, column, packed[:, level]))
    packed = lax.fori_loop(0, order, advance, square)
    return (jnp.tril(packed, -1) + jnp.eye(order, dtype=square.dtype), jnp.triu(packed))

def split_triangles(square):
    order = square.shape[0]
    width = min(order, 16)
    packed = square
    for start in range(0, order, width):
        finish = start + width
        lower_block, upper_block = small_factors(packed[start:finish, start:finish])
        packed = packed.at[start:finish, start:finish].set(jnp.tril(lower_block, -1) + upper_block)
        if finish < order:
            below = packed[finish:, start:finish]
            right = packed[start:finish, finish:]
            column_part = jax.scipy.linalg.solve_triangular(upper_block.T, below.T, lower=True).T
            row_part = jax.scipy.linalg.solve_triangular(lower_block, right, lower=True, unit_diagonal=True)
            packed = packed.at[finish:, start:finish].set(column_part)
            packed = packed.at[start:finish, finish:].set(row_part)
            packed = packed.at[finish:, finish:].set(packed[finish:, finish:] - product(column_part, row_part))
    unit_lower = jnp.tril(packed, -1) + jnp.eye(order, dtype=square.dtype)
    return (unit_lower, jnp.triu(packed))

def reference(matrix):
    panel_cols = matrix[:, :B]
    trailing = matrix[:, B:]
    orthogonal, upper_raw = jnp.linalg.qr(panel_cols)
    diag_signs = jnp.sign(jnp.diagonal(upper_raw))
    orthogonal = orthogonal * diag_signs[None, :]
    factor_r = upper_raw * diag_signs[:, None]
    identity = jnp.eye(B, dtype=matrix.dtype)
    unit_lower, upper_part = split_triangles(orthogonal[:B] + identity)
    upper_inverse = jax.scipy.linalg.solve_triangular(upper_part, identity, lower=False)
    lower_rows = product(orthogonal[B:], upper_inverse)
    reflectors = jnp.concatenate([unit_lower, lower_rows], axis=0)
    t_factor = jax.scipy.linalg.solve_triangular(unit_lower, upper_part.T, lower=True, unit_diagonal=True).T
    projected = product(reflectors.T, trailing)
    weights = product(t_factor.T, projected)
    updated = trailing - product(reflectors, weights)
    top_rows = jnp.triu(-factor_r) + jnp.tril(unit_lower, -1)
    panel_out = jnp.concatenate([top_rows, lower_rows], axis=0)
    return (jnp.concatenate([panel_out, updated], axis=1), t_factor)
```

```python
import functools
import jax
import jax.numpy as jnp
from jax import lax
from jax.experimental import pallas as pl
from jax.experimental.pallas import tpu as pltpu
from jax.sharding import PartitionSpec as P

B = 128
NB = 8
F32 = jnp.float32
BF16 = jnp.bfloat16
HI = lax.Precision.HIGHEST


def split3(x):
    h = x.astype(BF16).astype(F32)
    r = x - h
    m = r.astype(BF16).astype(F32)
    return h, m, r - m


def outer8(left, right):
    lh, lm, ll = split3(left)
    rh, rm, rl = split3(right)
    lhs = jnp.concatenate([lh, lh, lm, lm, lh, ll], axis=0).astype(BF16)
    rhs = jnp.concatenate([rh, rm, rh, rm, rl, rh], axis=0).astype(BF16)
    return lax.dot_general(lhs, rhs, (((0,), (0,)), ((), ())), preferred_element_type=F32)


def iotas():
    return (lax.broadcasted_iota(jnp.int32, (NB, B), 0), lax.broadcasted_iota(jnp.int32, (NB, B), 1))


def column(x, k0, i):
    return jnp.take_along_axis(x, jnp.full((NB, B), k0 + i, jnp.int32), axis=1, mode="promise_in_bounds")


def chol_block(k0, ga, r_out):
    row, lane = iotas()
    g = ga[pl.ds(k0, NB), :B]
    y = ga[pl.ds(k0, NB), B:]
    c = [column(g, k0, i) for i in range(NB)]
    ps = jnp.ones((NB, B), F32)
    pt = jnp.ones((NB, B), F32)
    cols = []
    for i in range(NB):
        p = jnp.broadcast_to(c[i][i:i + 1, :], (NB, B))
        m = jnp.where(row > i, c[i] * (1.0 / p), 0.0)
        ps = jnp.where(row == i, p, ps)
        cols.append((c[i], p))
        for a in range(i + 1, NB):
            c[a] = c[a] - m * c[a][i:i + 1, :]
        g, y = g - m * g[i:i + 1, :], y - m * y[i:i + 1, :]
    rs = root(ps)
    rb = jnp.where(lane >= k0 + row, g * rs, 0.0)
    yb = y * rs
    cr = [jnp.where(row <= i, c[i] * rs, 0.0) for i in range(NB)]
    rt = jnp.zeros((NB, B), F32)
    ct = []
    for i in range(NB):
        v = jnp.where(row >= i, cols[i][0] * jnp.broadcast_to(rs[i:i + 1, :], (NB, B)), 0.0)
        ct.append(v)
        rt = jnp.where(lane == k0 + i, v, rt)
    r_out[pl.ds(k0, NB), :] = rb
    ga[...] -= outer8(rb, jnp.concatenate([rb, yb], axis=1))
    return rb, yb, rt, tuple(cr), tuple(ct)


def root(x):
    r = lax.rsqrt(x)
    return r * (1.5 - 0.5 * x * r * r)


def lu_block(k0, rb, yb, rt, cr, crt, kb, kt, lt_out, u_out, z_out):
    row, lane = iotas()
    kr0 = kb[pl.ds(k0, NB), :B]
    kc0 = kt[pl.ds(k0, NB), :]
    b = kb[pl.ds(k0, NB), B:] + yb
    c = [column(kr0, k0, i) + cr[i] for i in range(NB)]
    ct = [column(kc0, k0, i) + crt[i] for i in range(NB)]
    kr, kc = kr0 + rb, kc0 + rt
    e = jnp.where(lane == k0 + row, 1.0, 0.0).astype(F32)
    ps = jnp.ones((NB, B), F32)
    for i in range(NB):
        p = jnp.broadcast_to(c[i][i:i + 1, :], (NB, B))
        inv = 1.0 / p
        m = jnp.where(row > i, c[i] * inv, 0.0)
        mt = jnp.where(row > i, ct[i] * inv, 0.0)
        ps = jnp.where(row == i, inv, ps)
        for a in range(i + 1, NB):
            c[a] = c[a] - m * c[a][i:i + 1, :]
            ct[a] = ct[a] - mt * ct[a][i:i + 1, :]
        kr, b = kr - m * kr[i:i + 1, :], b - m * b[i:i + 1, :]
        kc, e = kc - mt * kc[i:i + 1, :], e - mt * e[i:i + 1, :]
    ub = jnp.where(lane >= k0 + row, kr, 0.0)
    l = kc * ps
    e = e * ps
    inside = (lane >= k0) & (lane < k0 + NB)
    lp = jnp.where(inside, -e, l)
    lt_out[pl.ds(k0, NB), :] = jnp.where(lane > k0 + row, l, jnp.where(lane == k0 + row, 1.0, 0.0))
    u_out[pl.ds(k0, NB), :] = ub
    z_out[pl.ds(k0, NB), :] = b
    kb[pl.ds(k0, NB), :] = jnp.zeros((NB, 2 * B), F32)
    kb[...] -= outer8(lp, jnp.concatenate([ub, b], axis=1))
    lanes = lax.broadcasted_iota(jnp.int32, (B, B), 1)
    kt[...] = jnp.where((lanes >= k0) & (lanes < k0 + NB), 0.0, kt[...]) - outer8(ub, lp)


def eye():
    return jnp.where(lax.broadcasted_iota(jnp.int32, (B, B), 0) == lax.broadcasted_iota(jnp.int32, (B, B), 1), 1.0, 0.0).astype(F32)


def dot3(a, b, dims):
    return lax.dot_general(a, b, (dims, ((), ())), precision=HI, preferred_element_type=F32)


ROWS_L = 1024
COLS_L = 1536
PIECE = 96
NP = 16
NQ = 16
NZ = 8
CHUNK = ROWS_L // NQ
TURNS = COLS_L // B


def remote(src, dst, send_sem, recv_sem, **where):
    return pltpu.make_async_remote_copy(src_ref=src, dst_ref=dst, send_sem=send_sem, recv_sem=recv_sem,
                                        device_id=where, device_id_type=pl.DeviceIdType.MESH)


def each(count, body, start=0):
    def step(d, carry):
        body(d)
        return carry
    lax.fori_loop(start, count, step, 0)


def gather_kernel(a_hbm, p_out, wt_out, r_out, top_out, t_out, ui_out,
                  p_v, stage, at_h, at_l, a1t, a1b, ph2, ct, pair, cwb, ccwb, gl, gbuf, gp, wt,
                  ga, kb, kt, lt_s, u_s, z_s,
                  a_sem, p_sem, o_sem, ps_send, pp_send, p_recv, g_send, g_recv, h_send, h_recv,
                  gp_send, gp_recv, ga_send, ga_recv, a1_send, a1_recv, pr_send, pr_recv,
                  cw_send, cw_recv, ccw_send, ccw_recv, wc_send, wd_send, wp_send, w_recv):
    r = lax.axis_index("prow")
    q = lax.axis_index("pcol")
    z, core = lax.div(r, 2), lax.rem(r, 2)
    up = 2 * lax.rem(z + 1, NZ) + core
    down = 2 * lax.rem(z + NZ - 1, NZ) + core
    other = 2 * z + 1 - core
    first_col, first_row = q == 0, r == 0

    barrier = pltpu.get_barrier_semaphore()

    def greet_row(d):
        pl.semaphore_signal(barrier, inc=1, device_id={"prow": lax.rem(r + d, NP)}, device_id_type=pl.DeviceIdType.MESH)

    def greet_col(d):
        pl.semaphore_signal(barrier, inc=1, device_id={"pcol": lax.rem(q + d, NQ)}, device_id_type=pl.DeviceIdType.MESH)

    def load_panel():
        return pltpu.make_async_copy(a_hbm.at[:, pl.ds(0, B)], p_v, p_sem)

    def load(j):
        return pltpu.make_async_copy(a_hbm.at[:, pl.ds(pl.multiple_of(j * B, B), B)], stage.at[j], a_sem.at[j])

    @pl.when(first_col)
    def _():
        load_panel().start()

    each(NQ, greet_col, 1)
    each(NP, greet_row, 1)
    each(TURNS, lambda j: load(j).start())
    pl.semaphore_wait(barrier, NP + NQ - 2)

    def rows_of(ref, j, count):
        return ref.at[pl.ds(pl.multiple_of(j * count, count), count)]

    def scatter(j):
        return remote(rows_of(p_v, j, CHUNK), rows_of(p_v, j, CHUNK), ps_send.at[j], p_recv.at[j], pcol=j)

    def spread(mine, j):
        return remote(rows_of(p_v, mine, CHUNK), rows_of(p_v, mine, CHUNK), pp_send.at[j], p_recv.at[mine], pcol=j)

    def give_gram(j):
        return remote(rows_of(gl, j, NB), gbuf.at[r], g_send.at[j], g_recv.at[r], prow=j)

    def give_top(j):
        return remote(rows_of(p_v, j, NB), gp.at[j, pl.ds(NB, NB)], h_send.at[j], h_recv, prow=j)

    def plane(j):
        return remote(gp.at[r], gp.at[r], gp_send.at[j], gp_recv, pcol=j)

    def column_gather(d):
        j = lax.rem(r + d, NP)
        return remote(gp.at[r], gp.at[r], ga_send.at[j], ga_recv.at[r], prow=j)

    def turn(j):
        load(j).wait()
        block = stage[j].T
        h = block.astype(BF16)
        at = pl.ds(pl.multiple_of(j * B, B), B)
        at_h[at, :] = h
        at_l[at, :] = (block - h.astype(F32)).astype(BF16)
        a1t[at, :] = block[:, :B]

    @pl.when(first_col)
    def _():
        load_panel().wait()
        each(NQ, lambda j: scatter(j).start(), 1)
        each(NQ, lambda j: spread(0, j).start(), 1)
        gl[...] = dot3(p_v[...], p_v[...], ((0,), (0,)))
        each(NP, lambda d: give_gram(lax.rem(r + d, NP)).start(), 1)
        gbuf[pl.ds(r, 1)] = gl[pl.ds(pl.multiple_of(r * NB, NB), NB), :][None]

        @pl.when(first_row)
        def _():
            each(NP, lambda j: give_top(j).start(), 1)
            gp[0, NB:, :] = p_v[:NB, :]

    @pl.when(jnp.logical_not(first_col))
    def _():
        scatter(q).wait_recv()

        def pass_on(d):
            j = lax.rem(q + d, NQ)

            @pl.when(j != 0)
            def _():
                spread(q, j).start()

        each(NQ, pass_on, 1)

    each(TURNS // 2, turn)

    @pl.when(first_col)
    def _():
        def arrive(d):
            j = lax.rem(r + d, NP)
            remote(gbuf.at[j], gbuf.at[j], g_send.at[j], g_recv.at[j], prow=j).wait_recv()

        each(NP, arrive, 1)

        @pl.when(jnp.logical_not(first_row))
        def _():
            give_top(r).wait_recv()

        total = gbuf[0]
        for j in range(1, NP):
            total = total + gbuf[j]
        gp[pl.ds(r, 1), :NB, :] = total[None]
        each(NQ, lambda j: plane(j).start(), 1)

    @pl.when(jnp.logical_not(first_col))
    def _():
        plane(q).wait_recv()

    each(NP, lambda d: column_gather(d).start(), 1)
    each(TURNS, turn, TURNS // 2)

    def owner(j):
        return lax.rem(j, 2) * NZ + lax.div(j, 2)

    def give_a1(j):
        return remote(a1t.at[pl.ds(pl.multiple_of(owner(j) * PIECE, NB), PIECE)], a1b, a1_send.at[j], a1_recv, prow=j)

    @pl.when(first_row)
    def _():
        each(NP, lambda j: give_a1(j).start(), 1)
        a1b[...] = a1t[:PIECE, :]

    @pl.when(jnp.logical_not(first_col))
    def _():
        def arrive(d):
            j = lax.rem(q + d, NQ)
            remote(rows_of(p_v, j, CHUNK), rows_of(p_v, j, CHUNK), pp_send.at[j], p_recv.at[j], pcol=j).wait_recv()

        each(NQ, arrive, 1)

    keep_panel = pltpu.make_async_copy(p_v, p_out, o_sem.at[0])
    keep_panel.start()
    panel = p_v[...]
    ph = panel.astype(BF16)
    ph2[:, :B] = ph
    ph2[:, B:] = (panel - ph.astype(F32)).astype(BF16)

    def inner(start):
        def body(j):
            at = pl.ds(pl.multiple_of(start + j * B, B), B)
            both = jnp.dot(at_h[at, :], ph2[...], preferred_element_type=F32)
            low = jnp.dot(at_l[at, :], ph2[:, :B], preferred_element_type=F32)
            ct[at, :] = both[:, :B] + (both[:, B:] + low)
        return body

    half = NZ * PIECE
    theirs, ours = pl.multiple_of((1 - core) * half, half), pl.multiple_of(core * half, half)
    each(half // B, inner(theirs))
    swap = remote(ct.at[pl.ds(theirs, half)], pair, pr_send, pr_recv, prow=other)
    swap.start()
    each(half // B, inner(ours))

    def arrive_gram(d):
        j = lax.rem(r + d, NP)
        remote(gp.at[j], gp.at[j], ga_send.at[j], ga_recv.at[j], prow=j).wait_recv()

    each(NP, arrive_gram, 1)
    for j in range(NP):
        ga[NB * j:NB * (j + 1), :B] = gp[j, :NB, :]
        kb[NB * j:NB * (j + 1), :B] = gp[j, NB:, :]
    ga[:, B:] = eye()
    kb[:, B:] = jnp.zeros((B, B), F32)
    kt[...] = kb[:, :B].T

    def part(to):
        return pl.ds(pl.multiple_of(lax.rem(to + NZ, NZ) * PIECE, NB), PIECE)

    def send_up(s):
        return remote(pair.at[part(z + 5 - s)], cwb.at[s - 1], cw_send.at[s - 1], cw_recv.at[s - 1], prow=up)

    def send_down(s):
        return remote(pair.at[part(z - 4 + s)], ccwb.at[s - 1], ccw_send.at[s - 1], ccw_recv.at[s - 1], prow=down)

    def hop(s):
        if s == 0:
            swap.wait()
            pair[...] += ct[pl.ds(ours, half), :]
        else:
            send_up(s).wait_recv()
            pair[part(z + 4 - s), :] += cwb[s - 1]
            if s <= 3:
                send_down(s).wait_recv()
                pair[part(z - 3 + s), :] += ccwb[s - 1]
        if s < 4:
            send_up(s + 1).start()
        if s < 3:
            send_down(s + 1).start()

    state = chol_block(0, ga, r_out)

    def step(k, state):
        k0 = pl.multiple_of(k * NB, NB)
        lu_block(k0, *state, kb, kt, lt_s, u_s, z_s)
        return chol_block(pl.multiple_of(k0 + NB, NB), ga, r_out)

    for s in range(5):
        state = lax.fori_loop(3 * s, 3 * s + 3, step, state)
        hop(s)
    lu_block(B - NB, *state, kb, kt, lt_s, u_s, z_s)

    @pl.when(jnp.logical_not(first_row))
    def _():
        give_a1(r).wait_recv()

    m = kb[:, B:]
    total = pair[part(z), :] + dot3(a1b[...], r_out[...], ((1,), (0,)))
    mine = core * NZ + z
    wt[pl.ds(mine, 1)] = dot3(total, m, ((1,), (1,)))[None]

    def wsend(o, sem, to):
        return remote(wt.at[o], wt.at[o], sem, w_recv.at[o], prow=to)

    def wup(s):
        return wsend(core * NZ + lax.rem(z - s + NZ, NZ), wc_send.at[s], up)

    def wdown(s):
        return wsend(core * NZ + lax.rem(z + s, NZ), wd_send.at[s], down)

    def wacross(zz):
        return wsend(core * NZ + zz, wp_send.at[zz], other)

    wup(0).start()
    wdown(0).start()
    wacross(z).start()
    t_out[...] = dot3(u_s[...], z_s[...], ((1,), (1,)))
    ui_out[...] = dot3(m, dot3(r_out[...], lt_s[...], ((0,), (1,))), ((1,), (0,)))
    rows = lax.broadcasted_iota(jnp.int32, (B, B), 0)
    lanes = lax.broadcasted_iota(jnp.int32, (B, B), 1)
    top_out[...] = jnp.where(lanes >= rows, -r_out[...], lt_s[...].T)
    for s in range(1, 5):
        wup(s).wait_recv()
        if s < 4:
            wup(s).start()
        wacross(lax.rem(z - s + NZ, NZ)).start()
        if s < 4:
            wdown(s).wait_recv()
            if s < 3:
                wdown(s).start()
            wacross(lax.rem(z + s, NZ)).start()
    each(NZ, lambda zz: wsend((1 - core) * NZ + zz, wp_send.at[zz], other).wait_recv())
    keep = pltpu.make_async_copy(wt, wt_out, o_sem.at[1])
    keep.start()

    @pl.when(first_col)
    def _():
        each(NQ, lambda j: scatter(j).wait_send(), 1)
        each(NQ, lambda j: spread(0, j).wait_send(), 1)
        each(NP, lambda d: give_gram(lax.rem(r + d, NP)).wait_send(), 1)
        each(NQ, lambda j: plane(j).wait_send(), 1)

        @pl.when(first_row)
        def _():
            each(NP, lambda j: give_top(j).wait_send(), 1)

    @pl.when(jnp.logical_not(first_col))
    def _():
        def left(d):
            j = lax.rem(q + d, NQ)

            @pl.when(j != 0)
            def _():
                spread(q, j).wait_send()

        each(NQ, left, 1)

    @pl.when(first_row)
    def _():
        each(NP, lambda j: give_a1(j).wait_send(), 1)

    each(NP, lambda d: column_gather(d).wait_send(), 1)
    for s in range(4):
        send_up(s + 1).wait_send()
        wup(s).wait_send()
    for s in range(3):
        send_down(s + 1).wait_send()
        wdown(s).wait_send()
    each(NZ, lambda zz: wacross(zz).wait_send())
    keep_panel.wait()
    keep.wait()


def gather_call(matrix):
    sq = jax.ShapeDtypeStruct((B, B), F32)
    vm = pltpu.VMEM
    sem = pltpu.SemaphoreType.DMA
    anywhere = pl.BlockSpec(memory_space=pl.ANY)
    inside = pl.BlockSpec(memory_space=pltpu.VMEM)
    return pl.pallas_call(
        gather_kernel,
        out_shape=[jax.ShapeDtypeStruct((ROWS_L, B), F32), jax.ShapeDtypeStruct((NP, PIECE, B), F32)] + [sq] * 4,
        in_specs=[anywhere],
        out_specs=[anywhere, anywhere] + [inside] * 4,
        scratch_shapes=[
            vm((ROWS_L, B), F32), vm((TURNS, ROWS_L, B), F32), vm((COLS_L, ROWS_L), BF16), vm((COLS_L, ROWS_L), BF16),
            vm((COLS_L, B), F32), vm((PIECE, B), F32), vm((ROWS_L, 2 * B), BF16), vm((COLS_L, B), F32),
            vm((NZ * PIECE, B), F32), vm((4, PIECE, B), F32), vm((3, PIECE, B), F32), vm((B, B), F32),
            vm((NP, NB, B), F32), vm((NP, 2 * NB, B), F32), vm((NP, PIECE, B), F32),
            vm((B, 2 * B), F32), vm((B, 2 * B), F32), vm((B, B), F32), vm((B, B), F32), vm((B, B), F32), vm((B, B), F32),
            sem((TURNS,)), sem, sem((2,)), sem((NQ,)), sem((NQ,)), sem((NQ,)), sem((NP,)), sem((NP,)), sem((NP,)), sem,
            sem((NQ,)), sem, sem((NP,)), sem((NP,)), sem((NP,)), sem, sem, sem,
            sem((4,)), sem((4,)), sem((3,)), sem((3,)), sem((4,)), sem((3,)), sem((NZ,)), sem((NP,)),
        ],
        compiler_params=pltpu.CompilerParams(collective_id=0, has_side_effects=True, vmem_limit_bytes=40 * 2**20),
    )(matrix)


STRIP = 128


def update_kernel(flag, a_ref, p_ref, wt_ref, r_ref, top_ref, ui_ref, out_ref, w3):
    i = pl.program_id(0)

    @pl.when(i == 0)
    def _():
        w = wt_ref[...]
        h = w.astype(BF16)
        w3[:, :B] = h
        w3[:, B:2 * B] = (w - h.astype(F32)).astype(BF16)
        w3[:, 2 * B:] = h

    is_top = jnp.logical_and(flag[0] == 0, i == 0)
    plain = p_ref[...]
    p = plain + jnp.where(is_top, r_ref[...], 0.0)
    h = p.astype(BF16)
    left = jnp.concatenate([h, h, (p - h.astype(F32)).astype(BF16)], axis=1)
    gone = lax.dot_general(left, w3[...], (((1,), (1,)), ((), ())), preferred_element_type=F32)
    out_ref[...] = a_ref[...] - gone

    @pl.when(flag[1] == 0)
    def _():
        out_ref[:, :B] = jnp.where(is_top, top_ref[...], dot3(plain, ui_ref[...], ((1,), (0,))))


def update_call(flag, matrix, panel, wt, r, top, ui):
    whole = lambda shape: pl.BlockSpec(shape, lambda i: (0, 0))
    return pl.pallas_call(
        update_kernel,
        grid=(ROWS_L // STRIP,),
        out_shape=jax.ShapeDtypeStruct((ROWS_L, COLS_L), F32),
        in_specs=[pl.BlockSpec(memory_space=pltpu.SMEM), pl.BlockSpec((STRIP, COLS_L), lambda i: (i, 0)),
                  pl.BlockSpec((STRIP, B), lambda i: (i, 0)), whole((COLS_L, B)), whole((B, B)), whole((B, B)), whole((B, B))],
        out_specs=pl.BlockSpec((STRIP, COLS_L), lambda i: (i, 0)),
        scratch_shapes=[pltpu.VMEM((COLS_L, 3 * B), BF16)],
        compiler_params=pltpu.CompilerParams(vmem_limit_bytes=24 * 2**20),
    )(flag, matrix, panel, wt, r, top, ui)


def per_device(matrix):
    flag = jnp.stack([lax.axis_index("prow"), lax.axis_index("pcol")]).astype(jnp.int32)
    panel, wt, r, top, t, ui = gather_call(matrix)
    factored = update_call(flag, matrix, panel, wt.reshape(COLS_L, B), r, top, ui)
    return factored, t


def solution(mesh):
    return jax.shard_map(
        per_device,
        mesh=mesh,
        in_specs=(P("prow", "pcol"),),
        out_specs=(P("prow", "pcol"), P()),
        check_vma=False,
    )
```

```python
import functools
import jax
import jax.numpy as jnp
from jax import lax
from jax.experimental import pallas as pl
from jax.experimental.pallas import tpu as pltpu
from jax.sharding import PartitionSpec as P

B = 128
NB = 8
F32 = jnp.float32
BF16 = jnp.bfloat16
HI = lax.Precision.HIGHEST


def split3(x):
    h = x.astype(BF16).astype(F32)
    r = x - h
    m = r.astype(BF16).astype(F32)
    return h, m, r - m


def outer8(left, right):
    lh, lm, ll = split3(left)
    rh, rm, rl = split3(right)
    lhs = jnp.concatenate([lh, lh, lm, lm, lh, ll], axis=0).astype(BF16)
    rhs = jnp.concatenate([rh, rm, rh, rm, rl, rh], axis=0).astype(BF16)
    return lax.dot_general(lhs, rhs, (((0,), (0,)), ((), ())), preferred_element_type=F32)


def iotas():
    return (lax.broadcasted_iota(jnp.int32, (NB, B), 0), lax.broadcasted_iota(jnp.int32, (NB, B), 1))


def column(x, k0, i):
    return jnp.take_along_axis(x, jnp.full((NB, B), k0 + i, jnp.int32), axis=1, mode="promise_in_bounds")


def chol_block(k0, ga, r_out):
    row, lane = iotas()
    g = ga[pl.ds(k0, NB), :B]
    y = ga[pl.ds(k0, NB), B:]
    c = [column(g, k0, i) for i in range(NB)]
    ps = jnp.ones((NB, B), F32)
    pt = jnp.ones((NB, B), F32)
    cols = []
    for i in range(NB):
        p = jnp.broadcast_to(c[i][i:i + 1, :], (NB, B))
        m = jnp.where(row > i, c[i] * (1.0 / p), 0.0)
        ps = jnp.where(row == i, p, ps)
        cols.append((c[i], p))
        for a in range(i + 1, NB):
            c[a] = c[a] - m * c[a][i:i + 1, :]
        g, y = g - m * g[i:i + 1, :], y - m * y[i:i + 1, :]
    rs = root(ps)
    rb = jnp.where(lane >= k0 + row, g * rs, 0.0)
    yb = y * rs
    cr = [jnp.where(row <= i, c[i] * rs, 0.0) for i in range(NB)]
    rt = jnp.zeros((NB, B), F32)
    ct = []
    for i in range(NB):
        v = jnp.where(row >= i, cols[i][0] * jnp.broadcast_to(rs[i:i + 1, :], (NB, B)), 0.0)
        ct.append(v)
        rt = jnp.where(lane == k0 + i, v, rt)
    r_out[pl.ds(k0, NB), :] = rb
    ga[...] -= outer8(rb, jnp.concatenate([rb, yb], axis=1))
    return rb, yb, rt, tuple(cr), tuple(ct)


def root(x):
    r = lax.rsqrt(x)
    return r * (1.5 - 0.5 * x * r * r)


def lu_block(k0, rb, yb, rt, cr, crt, kb, kt, lt_out, u_out, z_out):
    row, lane = iotas()
    kr0 = kb[pl.ds(k0, NB), :B]
    kc0 = kt[pl.ds(k0, NB), :]
    b = kb[pl.ds(k0, NB), B:] + yb
    c = [column(kr0, k0, i) + cr[i] for i in range(NB)]
    ct = [column(kc0, k0, i) + crt[i] for i in range(NB)]
    kr, kc = kr0 + rb, kc0 + rt
    e = jnp.where(lane == k0 + row, 1.0, 0.0).astype(F32)
    ps = jnp.ones((NB, B), F32)
    for i in range(NB):
        p = jnp.broadcast_to(c[i][i:i + 1, :], (NB, B))
        inv = 1.0 / p
        m = jnp.where(row > i, c[i] * inv, 0.0)
        mt = jnp.where(row > i, ct[i] * inv, 0.0)
        ps = jnp.where(row == i, inv, ps)
        for a in range(i + 1, NB):
            c[a] = c[a] - m * c[a][i:i + 1, :]
            ct[a] = ct[a] - mt * ct[a][i:i + 1, :]
        kr, b = kr - m * kr[i:i + 1, :], b - m * b[i:i + 1, :]
        kc, e = kc - mt * kc[i:i + 1, :], e - mt * e[i:i + 1, :]
    ub = jnp.where(lane >= k0 + row, kr, 0.0)
    l = kc * ps
    e = e * ps
    inside = (lane >= k0) & (lane < k0 + NB)
    lp = jnp.where(inside, -e, l)
    lt_out[pl.ds(k0, NB), :] = jnp.where(lane > k0 + row, l, jnp.where(lane == k0 + row, 1.0, 0.0))
    u_out[pl.ds(k0, NB), :] = ub
    z_out[pl.ds(k0, NB), :] = b
    kb[pl.ds(k0, NB), :] = jnp.zeros((NB, 2 * B), F32)
    kb[...] -= outer8(lp, jnp.concatenate([ub, b], axis=1))
    lanes = lax.broadcasted_iota(jnp.int32, (B, B), 1)
    kt[...] = jnp.where((lanes >= k0) & (lanes < k0 + NB), 0.0, kt[...]) - outer8(ub, lp)


def eye():
    return jnp.where(lax.broadcasted_iota(jnp.int32, (B, B), 0) == lax.broadcasted_iota(jnp.int32, (B, B), 1), 1.0, 0.0).astype(F32)


def dot3(a, b, dims):
    return lax.dot_general(a, b, (dims, ((), ())), precision=HI, preferred_element_type=F32)


ROWS_L = 1024
COLS_L = 1536
PIECE = 96
NP = 16
NQ = 16
NZ = 8
CHUNK = ROWS_L // NQ
TURNS = COLS_L // B


def remote(src, dst, send_sem, recv_sem, **where):
    return pltpu.make_async_remote_copy(src_ref=src, dst_ref=dst, send_sem=send_sem, recv_sem=recv_sem,
                                        device_id=where, device_id_type=pl.DeviceIdType.MESH)


def each(count, body, start=0):
    def step(d, carry):
        body(d)
        return carry
    lax.fori_loop(start, count, step, 0)


GROUPS = 4
GROUP = ROWS_L // GROUPS
FAR = (4, 3, 5, 2, 6, 1, 7)
NEAR = (1, 7, 2, 6, 3, 5, 4)


def factor_kernel(a_hbm, out, t_out,
                  p_v, a_v, at_h, at_l, a1t, a1b, ph2, ct, pair, rsb, gl, gbuf, gp, wt, pk, v2,
                  ga, kb, kt, r_s, lt_s, u_s, z_s,
                  a_sem, p_sem, ps_send, pp_send, p_recv, g_send, g_recv, h_send, h_recv,
                  gp_send, gp_recv, ga_send, ga_recv, a1_send, a1_recv, pr_send, pr_recv,
                  rs_send, rs_recv, wd_send, wp_send, w_recv):
    r = lax.axis_index("prow")
    q = lax.axis_index("pcol")
    z, core = lax.div(r, 2), lax.rem(r, 2)
    other = 2 * z + 1 - core
    first_col, first_row = q == 0, r == 0

    barrier = pltpu.get_barrier_semaphore()

    def greet_row(d):
        pl.semaphore_signal(barrier, inc=1, device_id={"prow": lax.rem(r + d, NP)}, device_id_type=pl.DeviceIdType.MESH)

    def greet_col(d):
        pl.semaphore_signal(barrier, inc=1, device_id={"pcol": lax.rem(q + d, NQ)}, device_id_type=pl.DeviceIdType.MESH)

    def load_panel():
        return pltpu.make_async_copy(a_hbm.at[:, pl.ds(0, B)], p_v, p_sem)

    def load(j):
        at = pl.ds(pl.multiple_of(j * B, B), B)
        return pltpu.make_async_copy(a_hbm.at[:, at], a_v.at[:, at], a_sem.at[j])

    @pl.when(first_col)
    def _():
        load_panel().start()

    each(NQ, greet_col, 1)
    each(NP, greet_row, 1)
    each(TURNS, lambda j: load(j).start())
    pl.semaphore_wait(barrier, NP + NQ - 2)

    def rows_of(ref, j, count):
        return ref.at[pl.ds(pl.multiple_of(j * count, count), count)]

    def scatter(j):
        return remote(rows_of(p_v, j, CHUNK), rows_of(p_v, j, CHUNK), ps_send.at[j], p_recv.at[j], pcol=j)

    def spread_in(j):
        return remote(rows_of(p_v, j, CHUNK), rows_of(p_v, j, CHUNK), pp_send.at[j], p_recv.at[j], pcol=j)

    def spread(mine, j):
        return remote(rows_of(p_v, mine, CHUNK), rows_of(p_v, mine, CHUNK), pp_send.at[j], p_recv.at[mine], pcol=j)

    def give_gram(j):
        return remote(rows_of(gl, j, NB), gbuf.at[r], g_send.at[j], g_recv.at[r], prow=j)

    def give_top(j):
        return remote(rows_of(p_v, j, NB), gp.at[j, pl.ds(NB, NB)], h_send.at[j], h_recv, prow=j)

    def plane(j):
        return remote(gp.at[r], gp.at[r], gp_send.at[j], gp_recv, pcol=j)

    def column_gather(d):
        j = lax.rem(r + d, NP)
        return remote(gp.at[r], gp.at[r], ga_send.at[j], ga_recv.at[r], prow=j)

    def turn(j):
        load(j).wait()
        at = pl.ds(pl.multiple_of(j * B, B), B)
        block = a_v[:, at].T
        h = block.astype(BF16)
        at_h[at, :] = h
        at_l[at, :] = (block - h.astype(F32)).astype(BF16)
        a1t[at, :] = block[:, :B]

    @pl.when(first_col)
    def _():
        load_panel().wait()
        each(NQ, lambda j: scatter(j).start(), 1)
        each(NQ, lambda j: spread(0, j).start(), 1)
        gl[...] = dot3(p_v[...], p_v[...], ((0,), (0,)))
        each(NP, lambda d: give_gram(lax.rem(r + d, NP)).start(), 1)
        gbuf[pl.ds(r, 1)] = gl[pl.ds(pl.multiple_of(r * NB, NB), NB), :][None]

        @pl.when(first_row)
        def _():
            each(NP, lambda j: give_top(j).start(), 1)
            gp[0, NB:, :] = p_v[:NB, :]

    @pl.when(jnp.logical_not(first_col))
    def _():
        scatter(q).wait_recv()

        def pass_on(d):
            j = lax.rem(q + d, NQ)

            @pl.when(j != 0)
            def _():
                spread(q, j).start()

        each(NQ, pass_on, 1)

    each(TURNS // 2, turn)

    @pl.when(first_col)
    def _():
        def arrive(d):
            j = lax.rem(r + d, NP)
            remote(gbuf.at[j], gbuf.at[j], g_send.at[j], g_recv.at[j], prow=j).wait_recv()

        each(NP, arrive, 1)

        @pl.when(jnp.logical_not(first_row))
        def _():
            give_top(r).wait_recv()

        total = gbuf[0]
        for j in range(1, NP):
            total = total + gbuf[j]
        gp[pl.ds(r, 1), :NB, :] = total[None]
        each(NQ, lambda j: plane(j).start(), 1)
        each(NP, lambda d: column_gather(d).start(), 1)

    def give_a1(j):
        return remote(a1t.at[pl.ds(pl.multiple_of(j * PIECE, NB), PIECE)], a1b, a1_send.at[j], a1_recv, prow=j)

    each(TURNS, turn, TURNS // 2)

    @pl.when(first_row)
    def _():
        each(NP, lambda j: give_a1(j).start(), 1)
        a1b[...] = a1t[:PIECE, :]

    def group(step):
        return lax.rem(lax.div(q, GROUPS) + (0, 1, 3, 2)[step], GROUPS)

    def arrive_group(step):
        @pl.when(jnp.logical_not(first_col))
        def _():
            def arrive(d):
                j = group(step) * GROUPS + d

                @pl.when(j != q)
                def _():
                    spread_in(j).wait_recv()

            each(GROUPS, arrive)

        at = pl.ds(pl.multiple_of(group(step) * GROUP, GROUP), GROUP)
        panel = p_v[at, :]
        ph = panel.astype(BF16)
        ph2[:, :B] = ph
        ph2[:, B:] = (panel - ph.astype(F32)).astype(BF16)

    def inner(step):
        arrive_group(step)
        along = pl.ds(pl.multiple_of(group(step) * GROUP, GROUP), GROUP)
        both = jnp.dot(at_h[:, along], ph2[...], preferred_element_type=F32)
        low = jnp.dot(at_l[:, along], ph2[:, :B], preferred_element_type=F32)
        sums = both[:, :B] + (both[:, B:] + low)
        if step == 0:
            ct[...] = sums
        else:
            ct[...] += sums

    @pl.when(jnp.logical_not(first_col))
    def _():
        plane(q).wait_recv()
        each(NP, lambda d: column_gather(d).start(), 1)

    for step in range(GROUPS):
        inner(step)

    def ring(d):
        return lax.rem(z + d, NZ)

    def swap(to):
        theirs = pl.ds(pl.multiple_of((2 * to + 1 - core) * PIECE, 32), PIECE)
        return remote(ct.at[theirs], pair.at[to], pr_send.at[to], pr_recv.at[to], prow=other)

    def reduce_to(to):
        return remote(pair.at[to], rsb.at[z], rs_send.at[to], rs_recv.at[z], prow=2 * to + core)

    def far(d):
        return ring(jnp.where(d == NZ - 1, NZ, NZ // 2 + jnp.where(lax.rem(d, 2) == 0, 1, -1) * lax.div(d + 1, 2)))

    def ours_step(d):
        to = far(d)
        swap(to).wait_recv()
        pair[pl.ds(to, 1)] += ct[pl.ds(pl.multiple_of((2 * to + core) * PIECE, 32), PIECE), :][None]

        @pl.when(to != z)
        def _():
            reduce_to(to).start()

    each(NZ, lambda d: swap(far(d)).start())
    each(NZ, ours_step)

    def arrive_gram(d):
        j = lax.rem(r + d, NP)
        remote(gp.at[j], gp.at[j], ga_send.at[j], ga_recv.at[j], prow=j).wait_recv()

    each(NP, arrive_gram, 1)
    for j in range(NP):
        ga[NB * j:NB * (j + 1), :B] = gp[j, :NB, :]
        kb[NB * j:NB * (j + 1), :B] = gp[j, NB:, :]
    ga[:, B:] = eye()
    kb[:, B:] = jnp.zeros((B, B), F32)
    kt[...] = kb[:, :B].T

    state = chol_block(0, ga, r_s)

    def step(k, state):
        k0 = pl.multiple_of(k * NB, NB)
        lu_block(k0, *state, kb, kt, lt_s, u_s, z_s)
        return chol_block(pl.multiple_of(k0 + NB, NB), ga, r_s)

    state = lax.fori_loop(0, B // NB - 1, step, state)
    lu_block(B - NB, *state, kb, kt, lt_s, u_s, z_s)

    @pl.when(jnp.logical_not(first_row))
    def _():
        give_a1(r).wait_recv()

    m = kb[:, B:]
    total = pair[pl.ds(z, 1)][0] + dot3(a1b[...], r_s[...], ((1,), (0,)))
    for d in FAR:
        remote(rsb.at[ring(d)], rsb.at[ring(d)], rs_send.at[ring(d)], rs_recv.at[ring(d)], prow=r).wait_recv()
    for d in FAR:
        total = total + rsb[pl.ds(ring(d), 1)][0]
    wt[pl.ds(r, 1)] = dot3(total, m, ((1,), (1,)))[None]

    def wsend(o, sem, to):
        return remote(wt.at[o], wt.at[o], sem, w_recv.at[o], prow=to)

    def wout(d):
        return wsend(r, wd_send.at[d], 2 * ring(d) + core)

    def wacross(zz):
        return wsend(2 * zz + core, wp_send.at[zz], other)

    wacross(z).start()
    for d in (2, 6, 1, 7, 4, 3, 5):
        wout(d).start()

    t_out[...] = dot3(u_s[...], z_s[...], ((1,), (1,)))
    plain = p_v[...]
    p = jnp.concatenate([plain[:B] + jnp.where(first_row, r_s[...], 0.0), plain[B:]], axis=0)
    h = p.astype(BF16)
    pk[:, :B] = h
    pk[:, B:2 * B] = h
    pk[:, 2 * B:] = (p - h.astype(F32)).astype(BF16)

    @pl.when(first_col)
    def _():
        v2[...] = dot3(p_v[...], dot3(m, dot3(r_s[...], lt_s[...], ((0,), (1,))), ((1,), (0,))), ((1,), (0,)))

        @pl.when(first_row)
        def _():
            rows = lax.broadcasted_iota(jnp.int32, (B, B), 0)
            lanes = lax.broadcasted_iota(jnp.int32, (B, B), 1)
            v2[:B, :] = jnp.where(lanes >= rows, -r_s[...], lt_s[...].T)

    def come(o):
        wsend(o, wp_send.at[0], other).wait_recv()

    def come_and_pass(d):
        come(2 * ring(d) + core)
        wacross(ring(d)).start()

    def update(g):
        for zz in (2 * g, 2 * g + 1):
            come(2 * zz + 1 - core)
        w = wt[pl.ds(4 * g, 4)].reshape(4 * PIECE, B)
        wh = w.astype(BF16)
        w3 = jnp.concatenate([wh, (w - wh.astype(F32)).astype(BF16), wh], axis=1)
        cols = pl.ds(pl.multiple_of(g * 4 * PIECE, B), 4 * PIECE)

        out[:, cols] = a_v[:, cols] - lax.dot_general(
            pk[...], w3, (((1,), (1,)), ((), ())), preferred_element_type=F32)

    half, odd = lax.div(z, 2), lax.rem(z, 2)
    inner_group = lax.rem(half + 3 + 2 * odd, GROUPS)
    outer_group = lax.rem(half + 1 + 2 * odd, GROUPS)
    for d in (1, 7, 2, 6):
        come_and_pass(d)
    update(half)
    update(inner_group)
    for d in (3, 5):
        come_and_pass(d)
    update(outer_group)
    come_and_pass(4)
    update(lax.rem(half + 2, GROUPS))

    @pl.when(first_col)
    def _():
        out[:, :B] = v2[...]

    @pl.when(first_col)
    def _():
        each(NQ, lambda j: scatter(j).wait_send(), 1)
        each(NQ, lambda j: spread(0, j).wait_send(), 1)
        each(NP, lambda d: give_gram(lax.rem(r + d, NP)).wait_send(), 1)
        each(NQ, lambda j: plane(j).wait_send(), 1)

        @pl.when(first_row)
        def _():
            each(NP, lambda j: give_top(j).wait_send(), 1)

    @pl.when(jnp.logical_not(first_col))
    def _():
        def left(d):
            j = lax.rem(q + d, NQ)

            @pl.when(j != 0)
            def _():
                spread(q, j).wait_send()

        each(NQ, left, 1)

    @pl.when(first_row)
    def _():
        each(NP, lambda j: give_a1(j).wait_send(), 1)

    each(NP, lambda d: column_gather(d).wait_send(), 1)
    each(NZ, lambda to: swap(to).wait_send())
    for d in FAR:
        reduce_to(ring(d)).wait_send()
        wout(d).wait_send()
    each(NZ, lambda zz: wacross(zz).wait_send())


def factor_call(matrix):
    vm = pltpu.VMEM
    sem = pltpu.SemaphoreType.DMA
    square = vm((B, B), F32)
    return pl.pallas_call(
        factor_kernel,
        out_shape=[vm((ROWS_L, COLS_L), F32), vm((B, B), F32)],
        in_specs=[pl.BlockSpec(memory_space=pltpu.HBM)],
        out_specs=[pl.BlockSpec(memory_space=pltpu.VMEM)] * 2,
        scratch_shapes=[
            vm((ROWS_L, B), F32), vm((ROWS_L, COLS_L), F32), vm((COLS_L, ROWS_L), BF16), vm((COLS_L, ROWS_L), BF16),
            vm((COLS_L, B), F32), vm((PIECE, B), F32), vm((GROUP, 2 * B), BF16), vm((COLS_L, B), F32),
            vm((NZ, PIECE, B), F32), vm((NZ, PIECE, B), F32), square,
            vm((NP, NB, B), F32), vm((NP, 2 * NB, B), F32), vm((NP, PIECE, B), F32), vm((ROWS_L, 3 * B), BF16),
            vm((ROWS_L, B), F32),
            vm((B, 2 * B), F32), vm((B, 2 * B), F32), square, square, square, square, square,
            sem((TURNS,)), sem, sem((NQ,)), sem((NQ,)), sem((NQ,)), sem((NP,)), sem((NP,)),
            sem((NP,)), sem, sem((NQ,)), sem, sem((NP,)), sem((NP,)), sem((NP,)), sem, sem((NZ,)), sem((NZ,)),
            sem((NZ,)), sem((NZ,)), sem((NZ,)), sem((NZ,)), sem((NP,)),
        ],
        compiler_params=pltpu.CompilerParams(collective_id=0, has_side_effects=True, vmem_limit_bytes=40 * 2**20),
    )(pltpu.with_memory_space_constraint(matrix, pltpu.HBM))


PARTS = 8


def store_kernel(x, t, out, t_out, sem):
    copies = [pltpu.make_async_copy(t, t_out, sem.at[PARTS])]
    for i in range(PARTS):
        at = pl.ds(i * (ROWS_L // PARTS), ROWS_L // PARTS)
        copies.append(pltpu.make_async_copy(x.at[at], out.at[at], sem.at[i]))
    for copy in copies:
        copy.start()
    for copy in copies:
        copy.wait()


def store_call(x, t):
    return pl.pallas_call(
        store_kernel,
        out_shape=[pltpu.HBM(x.shape, F32), pltpu.HBM(t.shape, F32)],
        in_specs=[pl.BlockSpec(memory_space=pltpu.VMEM)] * 2,
        out_specs=[pl.BlockSpec(memory_space=pltpu.HBM)] * 2,
        scratch_shapes=[pltpu.SemaphoreType.DMA((PARTS + 1,))],
        compiler_params=pltpu.CompilerParams(vmem_limit_bytes=16 * 2**20),
    )(pltpu.with_memory_space_constraint(x, pltpu.VMEM), pltpu.with_memory_space_constraint(t, pltpu.VMEM))


def per_device(matrix):
    return tuple(store_call(*factor_call(matrix)))


def solution(mesh):
    return jax.shard_map(
        per_device,
        mesh=mesh,
        in_specs=(P("prow", "pcol"),),
        out_specs=(P("prow", "pcol"), P()),
        check_vma=False,
    )
```

```python
import functools
import jax
import jax.numpy as jnp
from jax import lax
from jax.experimental import pallas as pl
from jax.experimental.pallas import tpu as pltpu
from jax.sharding import PartitionSpec as P

B = 128
NB = 8
F32 = jnp.float32
BF16 = jnp.bfloat16
HI = lax.Precision.HIGHEST


def split3(x):
    h = x.astype(BF16).astype(F32)
    r = x - h
    m = r.astype(BF16).astype(F32)
    return h, m, r - m


def outer8(left, right):
    lh, lm, ll = split3(left)
    rh, rm, rl = split3(right)
    lhs = jnp.concatenate([lh, lh, lm, lm, lh, ll], axis=0).astype(BF16)
    rhs = jnp.concatenate([rh, rm, rh, rm, rl, rh], axis=0).astype(BF16)
    return lax.dot_general(lhs, rhs, (((0,), (0,)), ((), ())), preferred_element_type=F32)


def iotas():
    return (lax.broadcasted_iota(jnp.int32, (NB, B), 0), lax.broadcasted_iota(jnp.int32, (NB, B), 1))


def column(x, k0, i):
    return jnp.take_along_axis(x, jnp.full((NB, B), k0 + i, jnp.int32), axis=1, mode="promise_in_bounds")


def chol_block(k0, ga, r_out):
    row, lane = iotas()
    g = ga[pl.ds(k0, NB), :B]
    y = ga[pl.ds(k0, NB), B:]
    c = [column(g, k0, i) for i in range(NB)]
    ps = jnp.ones((NB, B), F32)
    pt = jnp.ones((NB, B), F32)
    cols = []
    for i in range(NB):
        p = jnp.broadcast_to(c[i][i:i + 1, :], (NB, B))
        m = jnp.where(row > i, c[i] * (1.0 / p), 0.0)
        ps = jnp.where(row == i, p, ps)
        cols.append((c[i], p))
        for a in range(i + 1, NB):
            c[a] = c[a] - m * c[a][i:i + 1, :]
        g, y = g - m * g[i:i + 1, :], y - m * y[i:i + 1, :]
    rs = root(ps)
    rb = jnp.where(lane >= k0 + row, g * rs, 0.0)
    yb = y * rs
    cr = [jnp.where(row <= i, c[i] * rs, 0.0) for i in range(NB)]
    rt = jnp.zeros((NB, B), F32)
    ct = []
    for i in range(NB):
        v = jnp.where(row >= i, cols[i][0] * jnp.broadcast_to(rs[i:i + 1, :], (NB, B)), 0.0)
        ct.append(v)
        rt = jnp.where(lane == k0 + i, v, rt)
    r_out[pl.ds(k0, NB), :] = rb
    ga[...] -= outer8(rb, jnp.concatenate([rb, yb], axis=1))
    return rb, yb, rt, tuple(cr), tuple(ct)


def root(x):
    r = lax.rsqrt(x)
    return r * (1.5 - 0.5 * x * r * r)


def lu_block(k0, rb, yb, rt, cr, crt, kb, kt, lt_out, u_out, z_out):
    row, lane = iotas()
    kr0 = kb[pl.ds(k0, NB), :B]
    kc0 = kt[pl.ds(k0, NB), :]
    b = kb[pl.ds(k0, NB), B:] + yb
    c = [column(kr0, k0, i) + cr[i] for i in range(NB)]
    ct = [column(kc0, k0, i) + crt[i] for i in range(NB)]
    kr, kc = kr0 + rb, kc0 + rt
    e = jnp.where(lane == k0 + row, 1.0, 0.0).astype(F32)
    ps = jnp.ones((NB, B), F32)
    for i in range(NB):
        p = jnp.broadcast_to(c[i][i:i + 1, :], (NB, B))
        inv = 1.0 / p
        m = jnp.where(row > i, c[i] * inv, 0.0)
        mt = jnp.where(row > i, ct[i] * inv, 0.0)
        ps = jnp.where(row == i, inv, ps)
        for a in range(i + 1, NB):
            c[a] = c[a] - m * c[a][i:i + 1, :]
            ct[a] = ct[a] - mt * ct[a][i:i + 1, :]
        kr, b = kr - m * kr[i:i + 1, :], b - m * b[i:i + 1, :]
        kc, e = kc - mt * kc[i:i + 1, :], e - mt * e[i:i + 1, :]
    ub = jnp.where(lane >= k0 + row, kr, 0.0)
    l = kc * ps
    e = e * ps
    inside = (lane >= k0) & (lane < k0 + NB)
    lp = jnp.where(inside, -e, l)
    lt_out[pl.ds(k0, NB), :] = jnp.where(lane > k0 + row, l, jnp.where(lane == k0 + row, 1.0, 0.0))
    u_out[pl.ds(k0, NB), :] = ub
    z_out[pl.ds(k0, NB), :] = b
    kb[pl.ds(k0, NB), :] = jnp.zeros((NB, 2 * B), F32)
    kb[...] -= outer8(lp, jnp.concatenate([ub, b], axis=1))
    lanes = lax.broadcasted_iota(jnp.int32, (B, B), 1)
    kt[...] = jnp.where((lanes >= k0) & (lanes < k0 + NB), 0.0, kt[...]) - outer8(ub, lp)


def eye():
    return jnp.where(lax.broadcasted_iota(jnp.int32, (B, B), 0) == lax.broadcasted_iota(jnp.int32, (B, B), 1), 1.0, 0.0).astype(F32)


def dot3(a, b, dims):
    return lax.dot_general(a, b, (dims, ((), ())), precision=HI, preferred_element_type=F32)


ROWS_L = 1024
COLS_L = 1536
PIECE = 96
NP = 16
NQ = 16
NZ = 8
CHUNK = ROWS_L // NQ
TURNS = COLS_L // B


def remote(src, dst, send_sem, recv_sem, **where):
    return pltpu.make_async_remote_copy(src_ref=src, dst_ref=dst, send_sem=send_sem, recv_sem=recv_sem,
                                        device_id=where, device_id_type=pl.DeviceIdType.MESH)


def each(count, body, start=0):
    def step(d, carry):
        body(d)
        return carry
    lax.fori_loop(start, count, step, 0)


GROUPS = 4
GROUP = ROWS_L // GROUPS
FAR = (4, 3, 5, 2, 6, 1, 7)
SENT = (2, 6, 1, 7)
FAR_ROWS = (8, 9, 7, 10, 6, 11, 5, 12, 4, 13, 3, 14, 2, 15, 1)
FAR_COLS = (10, 9, 11, 8, 6, 14, 5, 7, 13, 15, 4, 12, 2, 1, 3)


def factor_kernel(a_hbm, out, t_out,
                  p_v, a_v, at_h, at_l, a1t, a1b, ph2, ct, pair, rsb, gl, gbuf, gp, wt, pk, v2,
                  ga, kb, kt, r_s, lt_s, u_s, z_s,
                  a_sem, p_sem, ps_send, pp_send, p_recv, g_send, g_recv, h_send, h_recv,
                  gp_send, gp_recv, ga_send, ga_recv, a1_send, a1_recv, pr_send, pr_recv,
                  rs_send, rs_recv, wd_send, wp_send, w_recv, re_send, half_recv):
    r = lax.axis_index("prow")
    q = lax.axis_index("pcol")
    z, core = lax.div(r, 2), lax.rem(r, 2)
    other = 2 * z + 1 - core
    first_col, first_row = q == 0, r == 0

    barrier = pltpu.get_barrier_semaphore()

    def greet_row(d):
        pl.semaphore_signal(barrier, inc=1, device_id={"prow": lax.rem(r + d, NP)}, device_id_type=pl.DeviceIdType.MESH)

    def across_plane(d):
        return lax.rem(lax.div(q, 4) + d // 4, 4) * 4 + lax.rem(lax.rem(q, 4) + d % 4, 4)

    def greet_col(d):
        pl.semaphore_signal(barrier, inc=1, device_id={"pcol": across_plane(d)}, device_id_type=pl.DeviceIdType.MESH)

    def load_panel():
        return pltpu.make_async_copy(a_hbm.at[:, pl.ds(0, B)], p_v, p_sem)

    def load(j):
        at = pl.ds(pl.multiple_of(j * B, B), B)
        return pltpu.make_async_copy(a_hbm.at[:, at], a_v.at[:, at], a_sem.at[j])

    @pl.when(first_col)
    def _():
        load_panel().start()

    for d in FAR_COLS:
        greet_col(d)
    for d in FAR_ROWS:
        greet_row(d)
    each(TURNS, lambda j: load(j).start())
    pl.semaphore_wait(barrier, NP + NQ - 2)

    def rows_of(ref, j, count):
        return ref.at[pl.ds(pl.multiple_of(j * count, count), count)]

    def scatter(j):
        return remote(rows_of(p_v, j, CHUNK), rows_of(p_v, j, CHUNK), ps_send.at[j], p_recv.at[j], pcol=j)

    def spread_in(j):
        return remote(rows_of(p_v, j, CHUNK), rows_of(p_v, j, CHUNK), pp_send.at[j], p_recv.at[j], pcol=j)

    def spread(mine, j):
        return remote(rows_of(p_v, mine, CHUNK), rows_of(p_v, mine, CHUNK), pp_send.at[j], p_recv.at[mine], pcol=j)

    def give_gram(j):
        return remote(rows_of(gl, j, NB), gbuf.at[r], g_send.at[j], g_recv.at[r], prow=j)

    def give_top(j):
        return remote(rows_of(p_v, j, NB), gp.at[j, pl.ds(NB, NB)], h_send.at[j], h_recv, prow=j)

    def plane(j):
        return remote(gp.at[r], gp.at[r], gp_send.at[j], gp_recv, pcol=j)

    def column_gather(d):
        j = lax.rem(r + d, NP)
        return remote(gp.at[r], gp.at[r], ga_send.at[j], ga_recv.at[r], prow=j)

    def turn(j):
        load(j).wait()
        at = pl.ds(pl.multiple_of(j * B, B), B)
        block = a_v[:, at].T
        h = block.astype(BF16)
        at_h[at, :] = h
        at_l[at, :] = (block - h.astype(F32)).astype(BF16)
        a1t[at, :] = block[:, :B]

    @pl.when(first_col)
    def _():
        load_panel().wait()
        for j in FAR_COLS:
            scatter(j).start()
        gl[...] = dot3(p_v[...], p_v[...], ((0,), (0,)))
        for d in FAR_ROWS:
            give_gram(lax.rem(r + d, NP)).start()
        gbuf[pl.ds(r, 1)] = gl[pl.ds(pl.multiple_of(r * NB, NB), NB), :][None]

        @pl.when(first_row)
        def _():
            each(NP, lambda j: give_top(j).start(), 1)
            gp[0, NB:, :] = p_v[:NB, :]

    @pl.when(jnp.logical_not(first_col))
    def _():
        scatter(q).wait_recv()

        for d in FAR_COLS:
            j = across_plane(d)

            @pl.when(j != 0)
            def _():
                spread(q, j).start()

    each(TURNS // 2, turn)

    @pl.when(first_col)
    def _():
        def arrive(d):
            j = lax.rem(r + d, NP)
            remote(gbuf.at[j], gbuf.at[j], g_send.at[j], g_recv.at[j], prow=j).wait_recv()

        each(NP, arrive, 1)

        @pl.when(jnp.logical_not(first_row))
        def _():
            give_top(r).wait_recv()

        total = gbuf[0]
        for j in range(1, NP):
            total = total + gbuf[j]
        gp[pl.ds(r, 1), :NB, :] = total[None]
        for j in FAR_COLS:
            plane(j).start()
        for d in FAR_ROWS:
            column_gather(d).start()
        for j in FAR_COLS:
            spread(0, j).start()

    def give_a1(j):
        return remote(a1t.at[pl.ds(pl.multiple_of(j * PIECE, NB), PIECE)], a1b, a1_send.at[j], a1_recv, prow=j)

    each(TURNS, turn, TURNS // 2)

    @pl.when(first_row)
    def _():
        each(NP, lambda j: give_a1(j).start(), 1)
        a1b[...] = a1t[:PIECE, :]

    def group(step):
        return lax.rem(lax.div(q, GROUPS) + (2, 1, 3, 0)[step], GROUPS)

    def arrive_group(step):
        @pl.when(jnp.logical_not(first_col))
        def _():
            def arrive(d):
                j = group(step) * GROUPS + d

                @pl.when(j != q)
                def _():
                    spread_in(j).wait_recv()

            each(GROUPS, arrive)

        at = pl.ds(pl.multiple_of(group(step) * GROUP, GROUP), GROUP)
        panel = p_v[at, :]
        ph = panel.astype(BF16)
        ph2[:, :B] = ph
        ph2[:, B:] = (panel - ph.astype(F32)).astype(BF16)

    def inner(step):
        arrive_group(step)
        along = pl.ds(pl.multiple_of(group(step) * GROUP, GROUP), GROUP)
        both = jnp.dot(at_h[:, along], ph2[...], preferred_element_type=F32)
        low = jnp.dot(at_l[:, along], ph2[:, :B], preferred_element_type=F32)
        sums = both[:, :B] + (both[:, B:] + low)
        if step == 0:
            ct[...] = sums
        else:
            ct[...] += sums

    @pl.when(jnp.logical_not(first_col))
    def _():
        plane(q).wait_recv()
        for d in FAR_ROWS:
            column_gather(d).start()

    for step in range(GROUPS):
        inner(step)

    def ring(d):
        return lax.rem(z + d, NZ)

    def swap(to):
        theirs = pl.ds(pl.multiple_of((2 * to + 1 - core) * PIECE, 32), PIECE)
        return remote(ct.at[theirs], pair.at[to], pr_send.at[to], pr_recv.at[to], prow=other)

    def reduce_to(to):
        return remote(pair.at[to], rsb.at[z], rs_send.at[to], rs_recv.at[z], prow=2 * to + core)

    def far(d):
        return ring(jnp.where(d == NZ - 1, NZ, NZ // 2 + jnp.where(lax.rem(d, 2) == 0, 1, -1) * lax.div(d + 1, 2)))

    def ours_step(d):
        to = far(d)
        swap(to).wait_recv()
        pair[pl.ds(to, 1)] += ct[pl.ds(pl.multiple_of((2 * to + core) * PIECE, 32), PIECE), :][None]

        @pl.when(to != z)
        def _():
            reduce_to(to).start()

    each(NZ, lambda d: swap(far(d)).start())
    each(NZ, ours_step)

    def arrive_gram(d):
        j = lax.rem(r + d, NP)
        remote(gp.at[j], gp.at[j], ga_send.at[j], ga_recv.at[j], prow=j).wait_recv()

    each(NP, arrive_gram, 1)
    for j in range(NP):
        ga[NB * j:NB * (j + 1), :B] = gp[j, :NB, :]
        kb[NB * j:NB * (j + 1), :B] = gp[j, NB:, :]
    ga[:, B:] = eye()
    kb[:, B:] = jnp.zeros((B, B), F32)
    kt[...] = kb[:, :B].T

    state = chol_block(0, ga, r_s)

    def step(k, state):
        k0 = pl.multiple_of(k * NB, NB)
        lu_block(k0, *state, kb, kt, lt_s, u_s, z_s)
        return chol_block(pl.multiple_of(k0 + NB, NB), ga, r_s)

    state = lax.fori_loop(0, B // NB - 1, step, state)
    lu_block(B - NB, *state, kb, kt, lt_s, u_s, z_s)

    @pl.when(jnp.logical_not(first_row))
    def _():
        give_a1(r).wait_recv()

    m = kb[:, B:]
    total = pair[pl.ds(z, 1)][0] + dot3(a1b[...], r_s[...], ((1,), (0,)))
    for d in FAR:
        remote(rsb.at[ring(d)], rsb.at[ring(d)], rs_send.at[ring(d)], rs_recv.at[ring(d)], prow=r).wait_recv()
    for d in FAR:
        total = total + rsb[pl.ds(ring(d), 1)][0]
    wt[pl.ds(r, 1)] = dot3(total, m, ((1,), (1,)))[None]

    def wsend(o, sem, to):
        return remote(wt.at[o], wt.at[o], sem, w_recv.at[o], prow=to)

    def wout(d):
        return wsend(r, wd_send.at[d], 2 * ring(d) + core)

    def wacross(zz):
        return wsend(2 * zz + core, wp_send.at[zz], other)

    wacross(z).start()
    for d in SENT:
        wout(d).start()

    t_out[...] = dot3(u_s[...], z_s[...], ((1,), (1,)))
    plain = p_v[...]
    p = jnp.concatenate([plain[:B] + jnp.where(first_row, r_s[...], 0.0), plain[B:]], axis=0)
    h = p.astype(BF16)
    pk[:, :B] = h
    pk[:, B:2 * B] = h
    pk[:, 2 * B:] = (p - h.astype(F32)).astype(BF16)

    @pl.when(first_col)
    def _():
        v2[...] = dot3(p_v[...], dot3(m, dot3(r_s[...], lt_s[...], ((0,), (1,))), ((1,), (0,))), ((1,), (0,)))

        @pl.when(first_row)
        def _():
            rows = lax.broadcasted_iota(jnp.int32, (B, B), 0)
            lanes = lax.broadcasted_iota(jnp.int32, (B, B), 1)
            v2[:B, :] = jnp.where(lanes >= rows, -r_s[...], lt_s[...].T)

    halves = {2: pl.ds(0, PIECE // 2), 6: pl.ds(PIECE // 2, PIECE // 2)}

    def relay(d, k):
        o = 2 * ring(d) + core
        if k == 0:
            return wsend(o, re_send.at[d // 4], 2 * ring(7 if d == 2 else 1) + core)
        ref = wt.at[o, halves[d]]
        return remote(ref, ref, re_send.at[2 + d // 4], half_recv.at[d // 4], prow=2 * ring(8 - d) + core)

    def half_in(d):
        ref = wt.at[2 * ring(4) + core, halves[d]]
        return remote(ref, ref, re_send.at[2 + d // 4], half_recv.at[d // 4], prow=other)

    def come(o):
        wsend(o, wp_send.at[0], other).wait_recv()

    def come_and_pass(d):
        come(2 * ring(d) + core)
        wacross(ring(d)).start()

    def update(g):
        for zz in (2 * g, 2 * g + 1):
            come(2 * zz + 1 - core)
        w = wt[pl.ds(4 * g, 4)].reshape(4 * PIECE, B)
        wh = w.astype(BF16)
        w3 = jnp.concatenate([wh, (w - wh.astype(F32)).astype(BF16), wh], axis=1)
        cols = pl.ds(pl.multiple_of(g * 4 * PIECE, B), 4 * PIECE)

        out[:, cols] = a_v[:, cols] - lax.dot_general(
            pk[...], w3, (((1,), (1,)), ((), ())), preferred_element_type=F32)

    half, odd = lax.div(z, 2), lax.rem(z, 2)
    inner_group = lax.rem(half + 3 + 2 * odd, GROUPS)
    outer_group = lax.rem(half + 1 + 2 * odd, GROUPS)
    for d in (2, 6):
        come(2 * ring(d) + core)
        relay(d, 0).start()
        relay(d, 1).start()
        wacross(ring(d)).start()
    for d in (1, 7):
        come_and_pass(d)
    update(half)
    update(inner_group)
    for d in (3, 5):
        come_and_pass(d)
    for d in (2, 6):
        half_in(d).wait_recv()
    wacross(ring(4)).start()
    update(outer_group)
    update(lax.rem(half + 2, GROUPS))

    @pl.when(first_col)
    def _():
        out[:, :B] = v2[...]

    @pl.when(first_col)
    def _():
        each(NQ, lambda j: scatter(j).wait_send(), 1)
        each(NQ, lambda j: spread(0, j).wait_send(), 1)
        each(NP, lambda d: give_gram(lax.rem(r + d, NP)).wait_send(), 1)
        each(NQ, lambda j: plane(j).wait_send(), 1)

        @pl.when(first_row)
        def _():
            each(NP, lambda j: give_top(j).wait_send(), 1)

    @pl.when(jnp.logical_not(first_col))
    def _():
        def left(d):
            j = lax.rem(q + d, NQ)

            @pl.when(j != 0)
            def _():
                spread(q, j).wait_send()

        each(NQ, left, 1)

    @pl.when(first_row)
    def _():
        each(NP, lambda j: give_a1(j).wait_send(), 1)

    each(NP, lambda d: column_gather(d).wait_send(), 1)
    each(NZ, lambda to: swap(to).wait_send())
    for d in FAR:
        reduce_to(ring(d)).wait_send()
    for d in SENT:
        wout(d).wait_send()
    for d in (2, 6):
        relay(d, 0).wait_send()
        relay(d, 1).wait_send()
    each(NZ, lambda zz: wacross(zz).wait_send())


def factor_call(matrix):
    vm = pltpu.VMEM
    sem = pltpu.SemaphoreType.DMA
    square = vm((B, B), F32)
    return pl.pallas_call(
        factor_kernel,
        out_shape=[vm((ROWS_L, COLS_L), F32), vm((B, B), F32)],
        in_specs=[pl.BlockSpec(memory_space=pltpu.HBM)],
        out_specs=[pl.BlockSpec(memory_space=pltpu.VMEM)] * 2,
        scratch_shapes=[
            vm((ROWS_L, B), F32), vm((ROWS_L, COLS_L), F32), vm((COLS_L, ROWS_L), BF16), vm((COLS_L, ROWS_L), BF16),
            vm((COLS_L, B), F32), vm((PIECE, B), F32), vm((GROUP, 2 * B), BF16), vm((COLS_L, B), F32),
            vm((NZ, PIECE, B), F32), vm((NZ, PIECE, B), F32), square,
            vm((NP, NB, B), F32), vm((NP, 2 * NB, B), F32), vm((NP, PIECE, B), F32), vm((ROWS_L, 3 * B), BF16),
            vm((ROWS_L, B), F32),
            vm((B, 2 * B), F32), vm((B, 2 * B), F32), square, square, square, square, square,
            sem((TURNS,)), sem, sem((NQ,)), sem((NQ,)), sem((NQ,)), sem((NP,)), sem((NP,)),
            sem((NP,)), sem, sem((NQ,)), sem, sem((NP,)), sem((NP,)), sem((NP,)), sem, sem((NZ,)), sem((NZ,)),
            sem((NZ,)), sem((NZ,)), sem((NZ,)), sem((NZ,)), sem((NP,)), sem((4,)), sem((2,)),
        ],
        compiler_params=pltpu.CompilerParams(collective_id=0, has_side_effects=True, vmem_limit_bytes=40 * 2**20),
    )(pltpu.with_memory_space_constraint(matrix, pltpu.HBM))


PARTS = 8


def store_kernel(x, t, out, t_out, sem):
    copies = [pltpu.make_async_copy(t, t_out, sem.at[PARTS])]
    for i in range(PARTS):
        at = pl.ds(i * (ROWS_L // PARTS), ROWS_L // PARTS)
        copies.append(pltpu.make_async_copy(x.at[at], out.at[at], sem.at[i]))
    for copy in copies:
        copy.start()
    for copy in copies:
        copy.wait()


def store_call(x, t):
    return pl.pallas_call(
        store_kernel,
        out_shape=[pltpu.HBM(x.shape, F32), pltpu.HBM(t.shape, F32)],
        in_specs=[pl.BlockSpec(memory_space=pltpu.VMEM)] * 2,
        out_specs=[pl.BlockSpec(memory_space=pltpu.HBM)] * 2,
        scratch_shapes=[pltpu.SemaphoreType.DMA((PARTS + 1,))],
        compiler_params=pltpu.CompilerParams(vmem_limit_bytes=16 * 2**20),
    )(pltpu.with_memory_space_constraint(x, pltpu.VMEM), pltpu.with_memory_space_constraint(t, pltpu.VMEM))


def per_device(matrix):
    return tuple(store_call(*factor_call(matrix)))


def solution(mesh):
    return jax.shard_map(
        per_device,
        mesh=mesh,
        in_specs=(P("prow", "pcol"),),
        out_specs=(P("prow", "pcol"), P()),
        check_vma=False,
    )
```

```python
import functools
import jax
import jax.numpy as jnp
from jax import lax
from jax.experimental import pallas as pl
from jax.experimental.pallas import tpu as pltpu
from jax.sharding import PartitionSpec as P

B = 128
NB = 8
F32 = jnp.float32
BF16 = jnp.bfloat16
HI = lax.Precision.HIGHEST


def split3(x):
    h = x.astype(BF16).astype(F32)
    r = x - h
    m = r.astype(BF16).astype(F32)
    return h, m, r - m


def outer8(left, right):
    lh, lm, ll = split3(left)
    rh, rm, rl = split3(right)
    lhs = jnp.concatenate([lh, lh, lm, lm, lh, ll], axis=0).astype(BF16)
    rhs = jnp.concatenate([rh, rm, rh, rm, rl, rh], axis=0).astype(BF16)
    return lax.dot_general(lhs, rhs, (((0,), (0,)), ((), ())), preferred_element_type=F32)


def iotas():
    return (lax.broadcasted_iota(jnp.int32, (NB, B), 0), lax.broadcasted_iota(jnp.int32, (NB, B), 1))


def column(x, k0, i):
    return jnp.take_along_axis(x, jnp.full((NB, B), k0 + i, jnp.int32), axis=1, mode="promise_in_bounds")


def chol_block(k0, ga, r_out):
    row, lane = iotas()
    g = ga[pl.ds(k0, NB), :B]
    y = ga[pl.ds(k0, NB), B:]
    c = [column(g, k0, i) for i in range(NB)]
    ps = jnp.ones((NB, B), F32)
    pt = jnp.ones((NB, B), F32)
    cols = []
    for i in range(NB):
        p = jnp.broadcast_to(c[i][i:i + 1, :], (NB, B))
        m = jnp.where(row > i, c[i] * (1.0 / p), 0.0)
        ps = jnp.where(row == i, p, ps)
        cols.append((c[i], p))
        for a in range(i + 1, NB):
            c[a] = c[a] - m * c[a][i:i + 1, :]
        g, y = g - m * g[i:i + 1, :], y - m * y[i:i + 1, :]
    rs = root(ps)
    rb = jnp.where(lane >= k0 + row, g * rs, 0.0)
    yb = y * rs
    cr = [jnp.where(row <= i, c[i] * rs, 0.0) for i in range(NB)]
    rt = jnp.zeros((NB, B), F32)
    ct = []
    for i in range(NB):
        v = jnp.where(row >= i, cols[i][0] * jnp.broadcast_to(rs[i:i + 1, :], (NB, B)), 0.0)
        ct.append(v)
        rt = jnp.where(lane == k0 + i, v, rt)
    r_out[pl.ds(k0, NB), :] = rb
    ga[...] -= outer8(rb, jnp.concatenate([rb, yb], axis=1))
    return rb, yb, rt, tuple(cr), tuple(ct)


def root(x):
    r = lax.rsqrt(x)
    return r * (1.5 - 0.5 * x * r * r)


def lu_block(k0, rb, yb, rt, cr, crt, kb, kt, lt_out, u_out, z_out):
    row, lane = iotas()
    kr0 = kb[pl.ds(k0, NB), :B]
    kc0 = kt[pl.ds(k0, NB), :]
    b = kb[pl.ds(k0, NB), B:] + yb
    c = [column(kr0, k0, i) + cr[i] for i in range(NB)]
    ct = [column(kc0, k0, i) + crt[i] for i in range(NB)]
    kr, kc = kr0 + rb, kc0 + rt
    e = jnp.where(lane == k0 + row, 1.0, 0.0).astype(F32)
    ps = jnp.ones((NB, B), F32)
    for i in range(NB):
        p = jnp.broadcast_to(c[i][i:i + 1, :], (NB, B))
        inv = 1.0 / p
        m = jnp.where(row > i, c[i] * inv, 0.0)
        mt = jnp.where(row > i, ct[i] * inv, 0.0)
        ps = jnp.where(row == i, inv, ps)
        for a in range(i + 1, NB):
            c[a] = c[a] - m * c[a][i:i + 1, :]
            ct[a] = ct[a] - mt * ct[a][i:i + 1, :]
        kr, b = kr - m * kr[i:i + 1, :], b - m * b[i:i + 1, :]
        kc, e = kc - mt * kc[i:i + 1, :], e - mt * e[i:i + 1, :]
    ub = jnp.where(lane >= k0 + row, kr, 0.0)
    l = kc * ps
    e = e * ps
    inside = (lane >= k0) & (lane < k0 + NB)
    lp = jnp.where(inside, -e, l)
    lt_out[pl.ds(k0, NB), :] = jnp.where(lane > k0 + row, l, jnp.where(lane == k0 + row, 1.0, 0.0))
    u_out[pl.ds(k0, NB), :] = ub
    z_out[pl.ds(k0, NB), :] = b
    kb[pl.ds(k0, NB), :] = jnp.zeros((NB, 2 * B), F32)
    kb[...] -= outer8(lp, jnp.concatenate([ub, b], axis=1))
    lanes = lax.broadcasted_iota(jnp.int32, (B, B), 1)
    kt[...] = jnp.where((lanes >= k0) & (lanes < k0 + NB), 0.0, kt[...]) - outer8(ub, lp)


def eye():
    return jnp.where(lax.broadcasted_iota(jnp.int32, (B, B), 0) == lax.broadcasted_iota(jnp.int32, (B, B), 1), 1.0, 0.0).astype(F32)


def dot3(a, b, dims):
    return lax.dot_general(a, b, (dims, ((), ())), precision=HI, preferred_element_type=F32)


ROWS_L = 1024
COLS_L = 1536
PIECE = 96
NP = 16
NQ = 16
NZ = 8
CHUNK = ROWS_L // NQ
TURNS = COLS_L // B


def remote(src, dst, send_sem, recv_sem, **where):
    return pltpu.make_async_remote_copy(src_ref=src, dst_ref=dst, send_sem=send_sem, recv_sem=recv_sem,
                                        device_id=where, device_id_type=pl.DeviceIdType.MESH)


def each(count, body, start=0):
    def step(d, carry):
        body(d)
        return carry
    lax.fori_loop(start, count, step, 0)


GROUPS = 4
GROUP = ROWS_L // GROUPS
SENT = (2, 6, 1, 7)
SUM_ORDER = (3, 5, 4, 1, 7, 2, 6, 0)
SUMMED = (4, 2, 6, 1, 7)
FAR_ROWS = (8, 9, 7, 10, 6, 11, 5, 12, 4, 13, 3, 14, 2, 15, 1)
FAR_COLS = (10, 9, 11, 8, 6, 14, 5, 7, 13, 15, 4, 12, 2, 1, 3)


def factor_kernel(a_hbm, out, t_out,
                  p_v, a_v, at_h, at_l, a1t, a1b, ph2, ct, pair, rsb, gl, gbuf, gp, wt, pk, v2,
                  ga, kb, kt, r_s, lt_s, u_s, z_s,
                  a_sem, p_sem, ps_send, pp_send, p_recv, g_send, g_recv, h_send, h_recv,
                  gp_send, gp_recv, ga_send, ga_recv, a1_send, a1_recv, pr_send, pr_recv,
                  rs_send, rs_recv, wd_send, wp_send, w_recv, re_send, half_recv,
                  lent, le_send, le_recv):
    r = lax.axis_index("prow")
    q = lax.axis_index("pcol")
    z, core = lax.div(r, 2), lax.rem(r, 2)
    other = 2 * z + 1 - core
    first_col, first_row = q == 0, r == 0

    barrier = pltpu.get_barrier_semaphore()

    def greet_row(d):
        pl.semaphore_signal(barrier, inc=1, device_id={"prow": lax.rem(r + d, NP)}, device_id_type=pl.DeviceIdType.MESH)

    def across_plane(d):
        return lax.rem(lax.div(q, 4) + d // 4, 4) * 4 + lax.rem(lax.rem(q, 4) + d % 4, 4)

    def greet_col(d):
        pl.semaphore_signal(barrier, inc=1, device_id={"pcol": across_plane(d)}, device_id_type=pl.DeviceIdType.MESH)

    def load_panel():
        return pltpu.make_async_copy(a_hbm.at[:, pl.ds(0, B)], p_v, p_sem)

    def load(j):
        at = pl.ds(pl.multiple_of(j * B, B), B)
        return pltpu.make_async_copy(a_hbm.at[:, at], a_v.at[:, at], a_sem.at[j])

    @pl.when(first_col)
    def _():
        load_panel().start()

    for d in FAR_COLS:
        greet_col(d)
    for d in FAR_ROWS:
        greet_row(d)
    each(TURNS, lambda j: load(j).start())
    pl.semaphore_wait(barrier, NP + NQ - 2)

    def rows_of(ref, j, count):
        return ref.at[pl.ds(pl.multiple_of(j * count, count), count)]

    def scatter(j):
        return remote(rows_of(p_v, j, CHUNK), rows_of(p_v, j, CHUNK), ps_send.at[j], p_recv.at[j], pcol=j)

    def spread_in(j):
        return remote(rows_of(p_v, j, CHUNK), rows_of(p_v, j, CHUNK), pp_send.at[j], p_recv.at[j], pcol=j)

    def spread(mine, j):
        return remote(rows_of(p_v, mine, CHUNK), rows_of(p_v, mine, CHUNK), pp_send.at[j], p_recv.at[mine], pcol=j)

    def give_gram(j):
        return remote(rows_of(gl, j, NB), gbuf.at[r], g_send.at[j], g_recv.at[r], prow=j)

    def give_top(j):
        return remote(rows_of(p_v, j, NB), gp.at[j, pl.ds(NB, NB)], h_send.at[j], h_recv, prow=j)

    def plane(j):
        return remote(gp.at[r], gp.at[r], gp_send.at[j], gp_recv, pcol=j)

    def column_gather(d):
        j = lax.rem(r + d, NP)
        return remote(gp.at[r], gp.at[r], ga_send.at[j], ga_recv.at[r], prow=j)

    def turn(j):
        load(j).wait()
        at = pl.ds(pl.multiple_of(j * B, B), B)
        block = a_v[:, at].T
        h = block.astype(BF16)
        at_h[at, :] = h
        at_l[at, :] = (block - h.astype(F32)).astype(BF16)
        a1t[at, :] = block[:, :B]

    @pl.when(first_col)
    def _():
        load_panel().wait()
        for j in FAR_COLS:
            scatter(j).start()
        gl[...] = dot3(p_v[...], p_v[...], ((0,), (0,)))
        for d in FAR_ROWS:
            give_gram(lax.rem(r + d, NP)).start()
        gbuf[pl.ds(r, 1)] = gl[pl.ds(pl.multiple_of(r * NB, NB), NB), :][None]

        @pl.when(first_row)
        def _():
            each(NP, lambda j: give_top(j).start(), 1)
            gp[0, NB:, :] = p_v[:NB, :]

    @pl.when(jnp.logical_not(first_col))
    def _():
        scatter(q).wait_recv()

        for d in FAR_COLS:
            j = across_plane(d)

            @pl.when(j != 0)
            def _():
                spread(q, j).start()

    each(TURNS // 2, turn)

    @pl.when(first_col)
    def _():
        def arrive(d):
            j = lax.rem(r + d, NP)
            remote(gbuf.at[j], gbuf.at[j], g_send.at[j], g_recv.at[j], prow=j).wait_recv()

        each(NP, arrive, 1)

        @pl.when(jnp.logical_not(first_row))
        def _():
            give_top(r).wait_recv()

        total = gbuf[0]
        for j in range(1, NP):
            total = total + gbuf[j]
        gp[pl.ds(r, 1), :NB, :] = total[None]
        for j in FAR_COLS:
            plane(j).start()
        for d in FAR_ROWS:
            column_gather(d).start()
        for j in FAR_COLS:
            spread(0, j).start()

    def give_a1(j):
        return remote(a1t.at[pl.ds(pl.multiple_of(j * PIECE, NB), PIECE)], a1b, a1_send.at[j], a1_recv, prow=j)

    each(TURNS, turn, TURNS // 2)

    @pl.when(first_row)
    def _():
        each(NP, lambda j: give_a1(j).start(), 1)
        a1b[...] = a1t[:PIECE, :]

    def group(step):
        return lax.rem(lax.div(q, GROUPS) + (2, 1, 3, 0)[step], GROUPS)

    def arrive_group(step):
        @pl.when(jnp.logical_not(first_col))
        def _():
            def arrive(d):
                j = group(step) * GROUPS + d

                @pl.when(j != q)
                def _():
                    spread_in(j).wait_recv()

            each(GROUPS, arrive)

        at = pl.ds(pl.multiple_of(group(step) * GROUP, GROUP), GROUP)
        panel = p_v[at, :]
        ph = panel.astype(BF16)
        ph2[:, :B] = ph
        ph2[:, B:] = (panel - ph.astype(F32)).astype(BF16)

    def inner(step):
        arrive_group(step)
        along = pl.ds(pl.multiple_of(group(step) * GROUP, GROUP), GROUP)
        both = jnp.dot(at_h[:, along], ph2[...], preferred_element_type=F32)
        low = jnp.dot(at_l[:, along], ph2[:, :B], preferred_element_type=F32)
        sums = both[:, :B] + (both[:, B:] + low)
        if step == 0:
            ct[...] = sums
        else:
            ct[...] += sums

    @pl.when(jnp.logical_not(first_col))
    def _():
        plane(q).wait_recv()
        for d in FAR_ROWS:
            column_gather(d).start()

    for step in range(GROUPS):
        inner(step)

    def ring(d):
        return lax.rem(z + d, NZ)

    def swap(to):
        theirs = pl.ds(pl.multiple_of((2 * to + 1 - core) * PIECE, 32), PIECE)
        return remote(ct.at[theirs], pair.at[to], pr_send.at[to], pr_recv.at[to], prow=other)

    def reduce_to(to):
        return remote(pair.at[to], rsb.at[z], rs_send.at[to], rs_recv.at[z], prow=2 * to + core)

    def lean(d):
        k = d // 4
        return remote(pair.at[ring(d)], lent.at[k], le_send.at[k], le_recv.at[k],
                      prow=2 * ring(1 if d == 3 else 7) + core)

    for d in SUM_ORDER:
        swap(ring(d)).start()
    for d in SUM_ORDER:
        to = ring(d)
        swap(to).wait_recv()
        pair[pl.ds(to, 1)] += ct[pl.ds(pl.multiple_of((2 * to + core) * PIECE, 32), PIECE), :][None]
        if d in (3, 5):
            lean(d).start()
        elif d in (4, 1, 7):
            reduce_to(to).start()

    def send_on():
        for d, k in ((2, 3), (6, 5)):
            lean(k).wait_recv()
            pair[pl.ds(ring(d), 1)] += lent[pl.ds(k // 4, 1)]
            reduce_to(ring(d)).start()

    def arrive_gram(d):
        j = lax.rem(r + d, NP)
        remote(gp.at[j], gp.at[j], ga_send.at[j], ga_recv.at[j], prow=j).wait_recv()

    each(NP, arrive_gram, 1)
    for j in range(NP):
        ga[NB * j:NB * (j + 1), :B] = gp[j, :NB, :]
        kb[NB * j:NB * (j + 1), :B] = gp[j, NB:, :]
    ga[:, B:] = eye()
    kb[:, B:] = jnp.zeros((B, B), F32)
    kt[...] = kb[:, :B].T

    state = chol_block(0, ga, r_s)

    def step(k, state):
        k0 = pl.multiple_of(k * NB, NB)
        lu_block(k0, *state, kb, kt, lt_s, u_s, z_s)
        return chol_block(pl.multiple_of(k0 + NB, NB), ga, r_s)

    state = lax.fori_loop(0, 7, step, state)
    send_on()
    state = lax.fori_loop(7, B // NB - 1, step, state)
    lu_block(B - NB, *state, kb, kt, lt_s, u_s, z_s)

    @pl.when(jnp.logical_not(first_row))
    def _():
        give_a1(r).wait_recv()

    m = kb[:, B:]
    total = pair[pl.ds(z, 1)][0] + dot3(a1b[...], r_s[...], ((1,), (0,)))
    for d in SUMMED:
        remote(rsb.at[ring(d)], rsb.at[ring(d)], rs_send.at[ring(d)], rs_recv.at[ring(d)], prow=r).wait_recv()
    for d in SUMMED:
        total = total + rsb[pl.ds(ring(d), 1)][0]
    wt[pl.ds(r, 1)] = dot3(total, m, ((1,), (1,)))[None]

    def wsend(o, sem, to):
        return remote(wt.at[o], wt.at[o], sem, w_recv.at[o], prow=to)

    def wout(d):
        return wsend(r, wd_send.at[d], 2 * ring(d) + core)

    def wacross(zz):
        return wsend(2 * zz + core, wp_send.at[zz], other)

    wacross(z).start()
    for d in SENT:
        wout(d).start()

    t_out[...] = dot3(u_s[...], z_s[...], ((1,), (1,)))
    plain = p_v[...]
    p = jnp.concatenate([plain[:B] + jnp.where(first_row, r_s[...], 0.0), plain[B:]], axis=0)
    h = p.astype(BF16)
    pk[:, :B] = h
    pk[:, B:2 * B] = h
    pk[:, 2 * B:] = (p - h.astype(F32)).astype(BF16)

    @pl.when(first_col)
    def _():
        v2[...] = dot3(p_v[...], dot3(m, dot3(r_s[...], lt_s[...], ((0,), (1,))), ((1,), (0,))), ((1,), (0,)))

        @pl.when(first_row)
        def _():
            rows = lax.broadcasted_iota(jnp.int32, (B, B), 0)
            lanes = lax.broadcasted_iota(jnp.int32, (B, B), 1)
            v2[:B, :] = jnp.where(lanes >= rows, -r_s[...], lt_s[...].T)

    halves = {2: pl.ds(0, PIECE // 2), 6: pl.ds(PIECE // 2, PIECE // 2)}

    def relay(d, k):
        o = 2 * ring(d) + core
        if k == 0:
            return wsend(o, re_send.at[d // 4], 2 * ring(7 if d == 2 else 1) + core)
        ref = wt.at[o, halves[d]]
        return remote(ref, ref, re_send.at[2 + d // 4], half_recv.at[d // 4], prow=2 * ring(8 - d) + core)

    def half_in(d):
        ref = wt.at[2 * ring(4) + core, halves[d]]
        return remote(ref, ref, re_send.at[2 + d // 4], half_recv.at[d // 4], prow=other)

    def come(o):
        wsend(o, wp_send.at[0], other).wait_recv()

    def come_and_pass(d):
        come(2 * ring(d) + core)
        wacross(ring(d)).start()

    def update(g):
        for zz in (2 * g, 2 * g + 1):
            come(2 * zz + 1 - core)
        w = wt[pl.ds(4 * g, 4)].reshape(4 * PIECE, B)
        wh = w.astype(BF16)
        w3 = jnp.concatenate([wh, (w - wh.astype(F32)).astype(BF16), wh], axis=1)
        cols = pl.ds(pl.multiple_of(g * 4 * PIECE, B), 4 * PIECE)

        out[:, cols] = a_v[:, cols] - lax.dot_general(
            pk[...], w3, (((1,), (1,)), ((), ())), preferred_element_type=F32)

    half, odd = lax.div(z, 2), lax.rem(z, 2)
    inner_group = lax.rem(half + 3 + 2 * odd, GROUPS)
    outer_group = lax.rem(half + 1 + 2 * odd, GROUPS)
    for d in (2, 6):
        come(2 * ring(d) + core)
        relay(d, 0).start()
        relay(d, 1).start()
        wacross(ring(d)).start()
    for d in (1, 7):
        come_and_pass(d)
    update(half)
    update(inner_group)
    for d in (3, 5):
        come_and_pass(d)
    for d in (2, 6):
        half_in(d).wait_recv()
    wacross(ring(4)).start()
    update(outer_group)
    update(lax.rem(half + 2, GROUPS))

    @pl.when(first_col)
    def _():
        out[:, :B] = v2[...]

    @pl.when(first_col)
    def _():
        each(NQ, lambda j: scatter(j).wait_send(), 1)
        each(NQ, lambda j: spread(0, j).wait_send(), 1)
        each(NP, lambda d: give_gram(lax.rem(r + d, NP)).wait_send(), 1)
        each(NQ, lambda j: plane(j).wait_send(), 1)

        @pl.when(first_row)
        def _():
            each(NP, lambda j: give_top(j).wait_send(), 1)

    @pl.when(jnp.logical_not(first_col))
    def _():
        def left(d):
            j = lax.rem(q + d, NQ)

            @pl.when(j != 0)
            def _():
                spread(q, j).wait_send()

        each(NQ, left, 1)

    @pl.when(first_row)
    def _():
        each(NP, lambda j: give_a1(j).wait_send(), 1)

    each(NP, lambda d: column_gather(d).wait_send(), 1)
    each(NZ, lambda to: swap(to).wait_send())
    for d in SUMMED:
        reduce_to(ring(d)).wait_send()
    for d in (3, 5):
        lean(d).wait_send()
    for d in SENT:
        wout(d).wait_send()
    for d in (2, 6):
        relay(d, 0).wait_send()
        relay(d, 1).wait_send()
    each(NZ, lambda zz: wacross(zz).wait_send())


def factor_call(matrix):
    vm = pltpu.VMEM
    sem = pltpu.SemaphoreType.DMA
    square = vm((B, B), F32)
    return pl.pallas_call(
        factor_kernel,
        out_shape=[vm((ROWS_L, COLS_L), F32), vm((B, B), F32)],
        in_specs=[pl.BlockSpec(memory_space=pltpu.HBM)],
        out_specs=[pl.BlockSpec(memory_space=pltpu.VMEM)] * 2,
        scratch_shapes=[
            vm((ROWS_L, B), F32), vm((ROWS_L, COLS_L), F32), vm((COLS_L, ROWS_L), BF16), vm((COLS_L, ROWS_L), BF16),
            vm((COLS_L, B), F32), vm((PIECE, B), F32), vm((GROUP, 2 * B), BF16), vm((COLS_L, B), F32),
            vm((NZ, PIECE, B), F32), vm((NZ, PIECE, B), F32), square,
            vm((NP, NB, B), F32), vm((NP, 2 * NB, B), F32), vm((NP, PIECE, B), F32), vm((ROWS_L, 3 * B), BF16),
            vm((ROWS_L, B), F32),
            vm((B, 2 * B), F32), vm((B, 2 * B), F32), square, square, square, square, square,
            sem((TURNS,)), sem, sem((NQ,)), sem((NQ,)), sem((NQ,)), sem((NP,)), sem((NP,)),
            sem((NP,)), sem, sem((NQ,)), sem, sem((NP,)), sem((NP,)), sem((NP,)), sem, sem((NZ,)), sem((NZ,)),
            sem((NZ,)), sem((NZ,)), sem((NZ,)), sem((NZ,)), sem((NP,)), sem((4,)), sem((2,)),
            vm((2, PIECE, B), F32), sem((2,)), sem((2,)),
        ],
        compiler_params=pltpu.CompilerParams(collective_id=0, has_side_effects=True, vmem_limit_bytes=40 * 2**20),
    )(pltpu.with_memory_space_constraint(matrix, pltpu.HBM))


PARTS = 8


def store_kernel(x, t, out, t_out, sem):
    copies = [pltpu.make_async_copy(t, t_out, sem.at[PARTS])]
    for i in range(PARTS):
        at = pl.ds(i * (ROWS_L // PARTS), ROWS_L // PARTS)
        copies.append(pltpu.make_async_copy(x.at[at], out.at[at], sem.at[i]))
    for copy in copies:
        copy.start()
    for copy in copies:
        copy.wait()


def store_call(x, t):
    return pl.pallas_call(
        store_kernel,
        out_shape=[pltpu.HBM(x.shape, F32), pltpu.HBM(t.shape, F32)],
        in_specs=[pl.BlockSpec(memory_space=pltpu.VMEM)] * 2,
        out_specs=[pl.BlockSpec(memory_space=pltpu.HBM)] * 2,
        scratch_shapes=[pltpu.SemaphoreType.DMA((PARTS + 1,))],
        compiler_params=pltpu.CompilerParams(vmem_limit_bytes=16 * 2**20),
    )(pltpu.with_memory_space_constraint(x, pltpu.VMEM), pltpu.with_memory_space_constraint(t, pltpu.VMEM))


def per_device(matrix):
    return tuple(store_call(*factor_call(matrix)))


def solution(mesh):
    return jax.shard_map(
        per_device,
        mesh=mesh,
        in_specs=(P("prow", "pcol"),),
        out_specs=(P("prow", "pcol"), P()),
        check_vma=False,
    )
```

```python
import functools
import jax
import jax.numpy as jnp
from jax import lax
from jax.experimental import pallas as pl
from jax.experimental.pallas import tpu as pltpu
from jax.sharding import PartitionSpec as P

B = 128
NB = 8
F32 = jnp.float32
BF16 = jnp.bfloat16
HI = lax.Precision.HIGHEST


def split3(x):
    h = x.astype(BF16).astype(F32)
    r = x - h
    m = r.astype(BF16).astype(F32)
    return h, m, r - m


def outer8(left, right):
    lh, lm, ll = split3(left)
    rh, rm, rl = split3(right)
    lhs = jnp.concatenate([lh, lh, lm, lm, lh, ll], axis=0).astype(BF16)
    rhs = jnp.concatenate([rh, rm, rh, rm, rl, rh], axis=0).astype(BF16)
    return lax.dot_general(lhs, rhs, (((0,), (0,)), ((), ())), preferred_element_type=F32)


def iotas():
    return (lax.broadcasted_iota(jnp.int32, (NB, B), 0), lax.broadcasted_iota(jnp.int32, (NB, B), 1))


def column(x, k0, i):
    return jnp.take_along_axis(x, jnp.full((NB, B), k0 + i, jnp.int32), axis=1, mode="promise_in_bounds")


def chol_block(k0, ga, r_out):
    row, lane = iotas()
    g = ga[pl.ds(k0, NB), :B]
    y = ga[pl.ds(k0, NB), B:]
    c = [column(g, k0, i) for i in range(NB)]
    ps = jnp.ones((NB, B), F32)
    pt = jnp.ones((NB, B), F32)
    cols = []
    for i in range(NB):
        p = jnp.broadcast_to(c[i][i:i + 1, :], (NB, B))
        m = jnp.where(row > i, c[i] * (1.0 / p), 0.0)
        ps = jnp.where(row == i, p, ps)
        cols.append((c[i], p))
        for a in range(i + 1, NB):
            c[a] = c[a] - m * c[a][i:i + 1, :]
        g, y = g - m * g[i:i + 1, :], y - m * y[i:i + 1, :]
    rs = root(ps)
    rb = jnp.where(lane >= k0 + row, g * rs, 0.0)
    yb = y * rs
    cr = [jnp.where(row <= i, c[i] * rs, 0.0) for i in range(NB)]
    rt = jnp.zeros((NB, B), F32)
    ct = []
    for i in range(NB):
        v = jnp.where(row >= i, cols[i][0] * jnp.broadcast_to(rs[i:i + 1, :], (NB, B)), 0.0)
        ct.append(v)
        rt = jnp.where(lane == k0 + i, v, rt)
    r_out[pl.ds(k0, NB), :] = rb
    ga[...] -= outer8(rb, jnp.concatenate([rb, yb], axis=1))
    return rb, yb, rt, tuple(cr), tuple(ct)


def root(x):
    r = lax.rsqrt(x)
    return r * (1.5 - 0.5 * x * r * r)


def lu_block(k0, rb, yb, rt, cr, crt, kb, kt, lt_out, u_out, z_out):
    row, lane = iotas()
    kr0 = kb[pl.ds(k0, NB), :B]
    kc0 = kt[pl.ds(k0, NB), :]
    b = kb[pl.ds(k0, NB), B:] + yb
    c = [column(kr0, k0, i) + cr[i] for i in range(NB)]
    ct = [column(kc0, k0, i) + crt[i] for i in range(NB)]
    kr, kc = kr0 + rb, kc0 + rt
    e = jnp.where(lane == k0 + row, 1.0, 0.0).astype(F32)
    ps = jnp.ones((NB, B), F32)
    for i in range(NB):
        p = jnp.broadcast_to(c[i][i:i + 1, :], (NB, B))
        inv = 1.0 / p
        m = jnp.where(row > i, c[i] * inv, 0.0)
        mt = jnp.where(row > i, ct[i] * inv, 0.0)
        ps = jnp.where(row == i, inv, ps)
        for a in range(i + 1, NB):
            c[a] = c[a] - m * c[a][i:i + 1, :]
            ct[a] = ct[a] - mt * ct[a][i:i + 1, :]
        kr, b = kr - m * kr[i:i + 1, :], b - m * b[i:i + 1, :]
        kc, e = kc - mt * kc[i:i + 1, :], e - mt * e[i:i + 1, :]
    ub = jnp.where(lane >= k0 + row, kr, 0.0)
    l = kc * ps
    e = e * ps
    inside = (lane >= k0) & (lane < k0 + NB)
    lp = jnp.where(inside, -e, l)
    lt_out[pl.ds(k0, NB), :] = jnp.where(lane > k0 + row, l, jnp.where(lane == k0 + row, 1.0, 0.0))
    u_out[pl.ds(k0, NB), :] = ub
    z_out[pl.ds(k0, NB), :] = b
    kb[pl.ds(k0, NB), :] = jnp.zeros((NB, 2 * B), F32)
    kb[...] -= outer8(lp, jnp.concatenate([ub, b], axis=1))
    lanes = lax.broadcasted_iota(jnp.int32, (B, B), 1)
    kt[...] = jnp.where((lanes >= k0) & (lanes < k0 + NB), 0.0, kt[...]) - outer8(ub, lp)


def eye():
    return jnp.where(lax.broadcasted_iota(jnp.int32, (B, B), 0) == lax.broadcasted_iota(jnp.int32, (B, B), 1), 1.0, 0.0).astype(F32)


def dot3(a, b, dims):
    return lax.dot_general(a, b, (dims, ((), ())), precision=HI, preferred_element_type=F32)


ROWS_L = 1024
COLS_L = 1536
PIECE = 96
NP = 16
NQ = 16
NZ = 8
CHUNK = ROWS_L // NQ
TURNS = COLS_L // B


def remote(src, dst, send_sem, recv_sem, **where):
    return pltpu.make_async_remote_copy(src_ref=src, dst_ref=dst, send_sem=send_sem, recv_sem=recv_sem,
                                        device_id=where, device_id_type=pl.DeviceIdType.MESH)


def each(count, body, start=0):
    def step(d, carry):
        body(d)
        return carry
    lax.fori_loop(start, count, step, 0)


GROUPS = 4
GROUP = ROWS_L // GROUPS
SENT = (2, 6, 1, 7)
SUM_ORDER = (3, 5, 4, 1, 7, 2, 6, 0)
SUMMED = (4, 2, 6, 1, 7)
FAR_ROWS = (8, 9, 7, 10, 6, 11, 5, 12, 4, 13, 3, 14, 2, 15, 1)
FAR_COLS = (10, 9, 11, 8, 6, 14, 5, 7, 13, 15, 4, 12, 2, 1, 3)


def factor_kernel(a_hbm, out, t_out,
                  p_v, a_v, at_h, at_l, a1t, a1b, ph2, ct, pair, rsb, gl, gbuf, gp, wt, pk, v2,
                  ga, kb, kt, r_s, lt_s, u_s, z_s,
                  a_sem, p_sem, ps_send, pp_send, p_recv, g_send, g_recv, h_send, h_recv,
                  gp_send, gp_recv, ga_send, ga_recv, a1_send, a1_recv, pr_send, pr_recv,
                  rs_send, rs_recv, wd_send, wp_send, w_recv, re_send, half_recv,
                  lent, le_send, le_recv):
    r = lax.axis_index("prow")
    q = lax.axis_index("pcol")
    z, core = lax.div(r, 2), lax.rem(r, 2)
    other = 2 * z + 1 - core
    first_col, first_row = q == 0, r == 0

    barrier = pltpu.get_barrier_semaphore()

    def greet_row(d):
        pl.semaphore_signal(barrier, inc=1, device_id={"prow": lax.rem(r + d, NP)}, device_id_type=pl.DeviceIdType.MESH)

    def across_plane(d):
        return lax.rem(lax.div(q, 4) + d // 4, 4) * 4 + lax.rem(lax.rem(q, 4) + d % 4, 4)

    def greet_col(d):
        pl.semaphore_signal(barrier, inc=1, device_id={"pcol": across_plane(d)}, device_id_type=pl.DeviceIdType.MESH)

    def load_panel(g):
        at = pl.ds(g * GROUP, GROUP)
        return pltpu.make_async_copy(a_hbm.at[at, pl.ds(0, B)], p_v.at[at], p_sem.at[g])

    def load(j):
        at = pl.ds(pl.multiple_of(j * B, B), B)
        return pltpu.make_async_copy(a_hbm.at[:, at], a_v.at[:, at], a_sem.at[j])

    @pl.when(first_col)
    def _():
        for g in (2, 1, 3, 0):
            load_panel(g).start()

    for d in FAR_COLS:
        greet_col(d)
    for d in FAR_ROWS:
        greet_row(d)
    each(TURNS, lambda j: load(j).start())
    pl.semaphore_wait(barrier, NP + NQ - 2)

    def rows_of(ref, j, count):
        return ref.at[pl.ds(pl.multiple_of(j * count, count), count)]

    def scatter(j):
        return remote(rows_of(p_v, j, CHUNK), rows_of(p_v, j, CHUNK), ps_send.at[j], p_recv.at[j], pcol=j)

    def spread_in(j):
        return remote(rows_of(p_v, j, CHUNK), rows_of(p_v, j, CHUNK), pp_send.at[j], p_recv.at[j], pcol=j)

    def spread(mine, j):
        return remote(rows_of(p_v, mine, CHUNK), rows_of(p_v, mine, CHUNK), pp_send.at[j], p_recv.at[mine], pcol=j)

    def give_gram(j):
        return remote(rows_of(gl, j, NB), gbuf.at[r], g_send.at[j], g_recv.at[r], prow=j)

    def give_top(j):
        return remote(rows_of(p_v, j, NB), gp.at[j, pl.ds(NB, NB)], h_send.at[j], h_recv, prow=j)

    def plane(j):
        return remote(gp.at[r], gp.at[r], gp_send.at[j], gp_recv, pcol=j)

    def column_gather(d):
        j = lax.rem(r + d, NP)
        return remote(gp.at[r], gp.at[r], ga_send.at[j], ga_recv.at[r], prow=j)

    def turn(j):
        load(j).wait()
        at = pl.ds(pl.multiple_of(j * B, B), B)
        block = a_v[:, at].T
        h = block.astype(BF16)
        at_h[at, :] = h
        at_l[at, :] = (block - h.astype(F32)).astype(BF16)
        a1t[at, :] = block[:, :B]

    @pl.when(first_col)
    def _():
        waited = set()
        for j in FAR_COLS:
            if j // GROUPS not in waited:
                load_panel(j // GROUPS).wait()
                waited.add(j // GROUPS)
            scatter(j).start()
        gl[...] = dot3(p_v[...], p_v[...], ((0,), (0,)))
        for d in FAR_ROWS:
            give_gram(lax.rem(r + d, NP)).start()
        gbuf[pl.ds(r, 1)] = gl[pl.ds(pl.multiple_of(r * NB, NB), NB), :][None]

        @pl.when(first_row)
        def _():
            each(NP, lambda j: give_top(j).start(), 1)
            gp[0, NB:, :] = p_v[:NB, :]

    @pl.when(jnp.logical_not(first_col))
    def _():
        scatter(q).wait_recv()

        for d in FAR_COLS:
            j = across_plane(d)

            @pl.when(j != 0)
            def _():
                spread(q, j).start()

    each(TURNS // 2, turn)

    @pl.when(first_col)
    def _():
        def arrive(d):
            j = lax.rem(r + d, NP)
            remote(gbuf.at[j], gbuf.at[j], g_send.at[j], g_recv.at[j], prow=j).wait_recv()

        each(NP, arrive, 1)

        @pl.when(jnp.logical_not(first_row))
        def _():
            give_top(r).wait_recv()

        total = gbuf[0]
        for j in range(1, NP):
            total = total + gbuf[j]
        gp[pl.ds(r, 1), :NB, :] = total[None]
        for j in FAR_COLS:
            plane(j).start()
        for d in FAR_ROWS:
            column_gather(d).start()
        for j in FAR_COLS:
            spread(0, j).start()

    def give_a1(j):
        return remote(a1t.at[pl.ds(pl.multiple_of(j * PIECE, NB), PIECE)], a1b, a1_send.at[j], a1_recv, prow=j)

    each(TURNS, turn, TURNS // 2)

    @pl.when(first_row)
    def _():
        each(NP, lambda j: give_a1(j).start(), 1)
        a1b[...] = a1t[:PIECE, :]

    def group(step):
        return lax.rem(lax.div(q, GROUPS) + (2, 1, 3, 0)[step], GROUPS)

    def arrive_group(step):
        @pl.when(jnp.logical_not(first_col))
        def _():
            def arrive(d):
                j = group(step) * GROUPS + d

                @pl.when(j != q)
                def _():
                    spread_in(j).wait_recv()

            each(GROUPS, arrive)

        at = pl.ds(pl.multiple_of(group(step) * GROUP, GROUP), GROUP)
        panel = p_v[at, :]
        ph = panel.astype(BF16)
        ph2[:, :B] = ph
        ph2[:, B:] = (panel - ph.astype(F32)).astype(BF16)

    def inner(step):
        arrive_group(step)
        along = pl.ds(pl.multiple_of(group(step) * GROUP, GROUP), GROUP)
        both = jnp.dot(at_h[:, along], ph2[...], preferred_element_type=F32)
        low = jnp.dot(at_l[:, along], ph2[:, :B], preferred_element_type=F32)
        sums = both[:, :B] + (both[:, B:] + low)
        if step == 0:
            ct[...] = sums
        else:
            ct[...] += sums

    @pl.when(jnp.logical_not(first_col))
    def _():
        plane(q).wait_recv()
        for d in FAR_ROWS:
            column_gather(d).start()

    for step in range(GROUPS):
        inner(step)

    def ring(d):
        return lax.rem(z + d, NZ)

    def swap(to):
        theirs = pl.ds(pl.multiple_of((2 * to + 1 - core) * PIECE, 32), PIECE)
        return remote(ct.at[theirs], pair.at[to], pr_send.at[to], pr_recv.at[to], prow=other)

    def reduce_to(to):
        return remote(pair.at[to], rsb.at[z], rs_send.at[to], rs_recv.at[z], prow=2 * to + core)

    def lean(d):
        k = d // 4
        return remote(pair.at[ring(d)], lent.at[k], le_send.at[k], le_recv.at[k],
                      prow=2 * ring(1 if d == 3 else 7) + core)

    for d in SUM_ORDER:
        swap(ring(d)).start()
    for d in SUM_ORDER:
        to = ring(d)
        swap(to).wait_recv()
        pair[pl.ds(to, 1)] += ct[pl.ds(pl.multiple_of((2 * to + core) * PIECE, 32), PIECE), :][None]
        if d in (3, 5):
            lean(d).start()
        elif d in (4, 1, 7):
            reduce_to(to).start()

    def send_on():
        for d, k in ((2, 3), (6, 5)):
            lean(k).wait_recv()
            pair[pl.ds(ring(d), 1)] += lent[pl.ds(k // 4, 1)]
            reduce_to(ring(d)).start()

    def arrive_gram(d):
        j = lax.rem(r + d, NP)
        remote(gp.at[j], gp.at[j], ga_send.at[j], ga_recv.at[j], prow=j).wait_recv()

    each(NP, arrive_gram, 1)
    for j in range(NP):
        ga[NB * j:NB * (j + 1), :B] = gp[j, :NB, :]
        kb[NB * j:NB * (j + 1), :B] = gp[j, NB:, :]
    ga[:, B:] = eye()
    kb[:, B:] = jnp.zeros((B, B), F32)
    kt[...] = kb[:, :B].T

    state = chol_block(0, ga, r_s)

    def step(k, state):
        k0 = pl.multiple_of(k * NB, NB)
        lu_block(k0, *state, kb, kt, lt_s, u_s, z_s)
        return chol_block(pl.multiple_of(k0 + NB, NB), ga, r_s)

    state = lax.fori_loop(0, 7, step, state)
    send_on()
    state = lax.fori_loop(7, B // NB - 1, step, state)
    lu_block(B - NB, *state, kb, kt, lt_s, u_s, z_s)

    @pl.when(jnp.logical_not(first_row))
    def _():
        give_a1(r).wait_recv()

    m = kb[:, B:]
    total = pair[pl.ds(z, 1)][0] + dot3(a1b[...], r_s[...], ((1,), (0,)))
    for d in SUMMED:
        remote(rsb.at[ring(d)], rsb.at[ring(d)], rs_send.at[ring(d)], rs_recv.at[ring(d)], prow=r).wait_recv()
    for d in SUMMED:
        total = total + rsb[pl.ds(ring(d), 1)][0]
    wt[pl.ds(r, 1)] = dot3(total, m, ((1,), (1,)))[None]

    def wsend(o, sem, to):
        return remote(wt.at[o], wt.at[o], sem, w_recv.at[o], prow=to)

    def wout(d):
        return wsend(r, wd_send.at[d], 2 * ring(d) + core)

    def wacross(zz):
        return wsend(2 * zz + core, wp_send.at[zz], other)

    wacross(z).start()
    for d in SENT:
        wout(d).start()

    t_out[...] = dot3(u_s[...], z_s[...], ((1,), (1,)))
    plain = p_v[...]
    p = jnp.concatenate([plain[:B] + jnp.where(first_row, r_s[...], 0.0), plain[B:]], axis=0)
    h = p.astype(BF16)
    pk[:, :B] = h
    pk[:, B:2 * B] = h
    pk[:, 2 * B:] = (p - h.astype(F32)).astype(BF16)

    @pl.when(first_col)
    def _():
        v2[...] = dot3(p_v[...], dot3(m, dot3(r_s[...], lt_s[...], ((0,), (1,))), ((1,), (0,))), ((1,), (0,)))

        @pl.when(first_row)
        def _():
            rows = lax.broadcasted_iota(jnp.int32, (B, B), 0)
            lanes = lax.broadcasted_iota(jnp.int32, (B, B), 1)
            v2[:B, :] = jnp.where(lanes >= rows, -r_s[...], lt_s[...].T)

    halves = {2: pl.ds(0, PIECE // 2), 6: pl.ds(PIECE // 2, PIECE // 2)}

    def relay(d, k):
        o = 2 * ring(d) + core
        if k == 0:
            return wsend(o, re_send.at[d // 4], 2 * ring(7 if d == 2 else 1) + core)
        ref = wt.at[o, halves[d]]
        return remote(ref, ref, re_send.at[2 + d // 4], half_recv.at[d // 4], prow=2 * ring(8 - d) + core)

    def half_in(d):
        ref = wt.at[2 * ring(4) + core, halves[d]]
        return remote(ref, ref, re_send.at[2 + d // 4], half_recv.at[d // 4], prow=other)

    def come(o):
        wsend(o, wp_send.at[0], other).wait_recv()

    def come_and_pass(d):
        come(2 * ring(d) + core)
        wacross(ring(d)).start()

    def update(g):
        for zz in (2 * g, 2 * g + 1):
            come(2 * zz + 1 - core)
        w = wt[pl.ds(4 * g, 4)].reshape(4 * PIECE, B)
        wh = w.astype(BF16)
        w3 = jnp.concatenate([wh, (w - wh.astype(F32)).astype(BF16), wh], axis=1)
        cols = pl.ds(pl.multiple_of(g * 4 * PIECE, B), 4 * PIECE)

        out[:, cols] = a_v[:, cols] - lax.dot_general(
            pk[...], w3, (((1,), (1,)), ((), ())), preferred_element_type=F32)

    half, odd = lax.div(z, 2), lax.rem(z, 2)
    inner_group = lax.rem(half + 3 + 2 * odd, GROUPS)
    outer_group = lax.rem(half + 1 + 2 * odd, GROUPS)
    for d in (2, 6):
        come(2 * ring(d) + core)
        relay(d, 0).start()
        relay(d, 1).start()
        wacross(ring(d)).start()
    for d in (1, 7):
        come_and_pass(d)
    update(half)
    update(inner_group)
    for d in (3, 5):
        come_and_pass(d)
    for d in (2, 6):
        half_in(d).wait_recv()
    wacross(ring(4)).start()
    update(outer_group)
    update(lax.rem(half + 2, GROUPS))

    @pl.when(first_col)
    def _():
        out[:, :B] = v2[...]

    @pl.when(first_col)
    def _():
        each(NQ, lambda j: scatter(j).wait_send(), 1)
        each(NQ, lambda j: spread(0, j).wait_send(), 1)
        each(NP, lambda d: give_gram(lax.rem(r + d, NP)).wait_send(), 1)
        each(NQ, lambda j: plane(j).wait_send(), 1)

        @pl.when(first_row)
        def _():
            each(NP, lambda j: give_top(j).wait_send(), 1)

    @pl.when(jnp.logical_not(first_col))
    def _():
        def left(d):
            j = lax.rem(q + d, NQ)

            @pl.when(j != 0)
            def _():
                spread(q, j).wait_send()

        each(NQ, left, 1)

    @pl.when(first_row)
    def _():
        each(NP, lambda j: give_a1(j).wait_send(), 1)

    each(NP, lambda d: column_gather(d).wait_send(), 1)
    each(NZ, lambda to: swap(to).wait_send())
    for d in SUMMED:
        reduce_to(ring(d)).wait_send()
    for d in (3, 5):
        lean(d).wait_send()
    for d in SENT:
        wout(d).wait_send()
    for d in (2, 6):
        relay(d, 0).wait_send()
        relay(d, 1).wait_send()
    each(NZ, lambda zz: wacross(zz).wait_send())


def factor_call(matrix):
    vm = pltpu.VMEM
    sem = pltpu.SemaphoreType.DMA
    square = vm((B, B), F32)
    return pl.pallas_call(
        factor_kernel,
        out_shape=[vm((ROWS_L, COLS_L), F32), vm((B, B), F32)],
        in_specs=[pl.BlockSpec(memory_space=pltpu.HBM)],
        out_specs=[pl.BlockSpec(memory_space=pltpu.VMEM)] * 2,
        scratch_shapes=[
            vm((ROWS_L, B), F32), vm((ROWS_L, COLS_L), F32), vm((COLS_L, ROWS_L), BF16), vm((COLS_L, ROWS_L), BF16),
            vm((COLS_L, B), F32), vm((PIECE, B), F32), vm((GROUP, 2 * B), BF16), vm((COLS_L, B), F32),
            vm((NZ, PIECE, B), F32), vm((NZ, PIECE, B), F32), square,
            vm((NP, NB, B), F32), vm((NP, 2 * NB, B), F32), vm((NP, PIECE, B), F32), vm((ROWS_L, 3 * B), BF16),
            vm((ROWS_L, B), F32),
            vm((B, 2 * B), F32), vm((B, 2 * B), F32), square, square, square, square, square,
            sem((TURNS,)), sem((GROUPS,)), sem((NQ,)), sem((NQ,)), sem((NQ,)), sem((NP,)), sem((NP,)),
            sem((NP,)), sem, sem((NQ,)), sem, sem((NP,)), sem((NP,)), sem((NP,)), sem, sem((NZ,)), sem((NZ,)),
            sem((NZ,)), sem((NZ,)), sem((NZ,)), sem((NZ,)), sem((NP,)), sem((4,)), sem((2,)),
            vm((2, PIECE, B), F32), sem((2,)), sem((2,)),
        ],
        compiler_params=pltpu.CompilerParams(collective_id=0, has_side_effects=True, vmem_limit_bytes=40 * 2**20),
    )(pltpu.with_memory_space_constraint(matrix, pltpu.HBM))


PARTS = 8


def store_kernel(x, t, out, t_out, sem):
    copies = [pltpu.make_async_copy(t, t_out, sem.at[PARTS])]
    for i in range(PARTS):
        at = pl.ds(i * (ROWS_L // PARTS), ROWS_L // PARTS)
        copies.append(pltpu.make_async_copy(x.at[at], out.at[at], sem.at[i]))
    for copy in copies:
        copy.start()
    for copy in copies:
        copy.wait()


def store_call(x, t):
    return pl.pallas_call(
        store_kernel,
        out_shape=[pltpu.HBM(x.shape, F32), pltpu.HBM(t.shape, F32)],
        in_specs=[pl.BlockSpec(memory_space=pltpu.VMEM)] * 2,
        out_specs=[pl.BlockSpec(memory_space=pltpu.HBM)] * 2,
        scratch_shapes=[pltpu.SemaphoreType.DMA((PARTS + 1,))],
        compiler_params=pltpu.CompilerParams(vmem_limit_bytes=16 * 2**20),
    )(pltpu.with_memory_space_constraint(x, pltpu.VMEM), pltpu.with_memory_space_constraint(t, pltpu.VMEM))


def per_device(matrix):
    return tuple(store_call(*factor_call(matrix)))


def solution(mesh):
    return jax.shard_map(
        per_device,
        mesh=mesh,
        in_specs=(P("prow", "pcol"),),
        out_specs=(P("prow", "pcol"), P()),
        check_vma=False,
    )
```
